512 devices in a mesh: node: 8 (over x, core), dev: 64 (over z, y).
Axes of the slice: x: 4, y: 4, z: 16, core: 2. Of those that a mesh axis runs over, the one named last changes fastest.
Arguments:
- element_load: float32 [16, 64, 8, 8, 8, 128], P('node', 'dev'), may hold values from -22 to 22
- orient: int32 [16, 64, 128], P('node', 'dev'), may hold values from 0 to 7
- size_x: float32 [16], P('node'), may hold values from 0.5 to 2
- size_y: float32 [64], P('dev'), may hold values from 0.5 to 2
- size_z: float32 [128], replicated, may hold values from 0.5 to 2
Outputs:
- solution: float32 [16, 64, 8, 8, 8, 128], P('node', 'dev')
- residual: float32 [16, 64, 8, 8, 8, 128], P('node', 'dev')
The draws below stay inside these ranges and needn't reach their ends.
All inputs are finite; a program needn't handle non-finite values.
Results may differ from the reference program's by a relative error of at most 0.019.
Values sent between devices are 32-bit elements; how exact they have to be, the bound alone decides.
No kernel may reach another device: no remote copies, remote signals or barrier semaphores. Data moves between devices by JAX's collectives and lax.ppermute only.
A program may use at most 64 MiB of HBM per device.

```python
import math
import jax
import jax.numpy as jnp
from jax import lax

POINTS = 8
EZ = 128
ITERS = 2
EXG = 16
EYG = 64


def draw_element_load(key, part):
    key = jax.random.fold_in(key, 11)
    shape_full = (EXG, EYG, POINTS, POINTS, POINTS, EZ)
    ramp_x = 1.0 + 0.8 * jnp.arange(EXG, dtype=jnp.float32) / (EXG - 1)
    ramp_y = 1.0 + 2.0 * jnp.arange(EYG, dtype=jnp.float32) / (EYG - 1)
    ramp_full = (ramp_x[:, None] * ramp_y[None, :])[:, :, None, None, None, None]
    values = jnp.clip(jax.random.normal(key, shape_full, jnp.float32), -4.0, 4.0)
    return values * ramp_full


def place_ends(entries, rng, low, top_value):
    longest = entries.shape.index(max(entries.shape))
    spots = []
    for shift in (0, 1):
        where = [jax.random.randint(jax.random.fold_in(rng, axis), (), 0, length) for axis, length in enumerate(entries.shape)]
        where[longest] = (where[longest] + shift) % entries.shape[longest]
        spots.append(tuple(where))
    return entries.at[spots[0]].set(low).at[spots[1]].set(top_value)


def level_of(stream_key, dims, shards, low, largest):
    def one(dim, parts):
        steps = jax.random.uniform(jax.random.fold_in(jax.random.fold_in(stream_key, 6), dim), (parts,), jnp.float32, low / len(shards), largest / len(shards))
        return jnp.repeat(jnp.exp(steps), dims[dim] // parts).reshape((-1,) + (1,) * (len(dims) - dim - 1))

    gain = one(*shards[0])
    for cut in shards[1:]:
        gain = gain * one(*cut)
    return gain


def setup_inputs(seed: int = 0) -> dict:
    arg_keys = jax.random.split(jax.random.key(seed), 6)
    element_load = draw_element_load(jax.random.fold_in(arg_keys[5], 71), 0)
    orient = place_ends(jax.random.randint(arg_keys[1], (EXG, EYG, EZ), 0, 8), jax.random.fold_in(arg_keys[1], 1), 0, 7).astype(jnp.int32)
    size_x = jnp.clip(jnp.exp(math.log(2.0) - 1.3862944 * jax.random.uniform(arg_keys[2], (EXG,), jnp.float32) ** level_of(arg_keys[2], (EXG,), ((0, 8),), -0.2, 0.2)), 0.5, 2.0)
    size_y = jnp.clip(jnp.exp(math.log(2.0) - 1.3862944 * jax.random.uniform(arg_keys[3], (EYG,), jnp.float32) ** level_of(arg_keys[3], (EYG,), ((0, 64),), -0.2, 0.2)), 0.5, 2.0)
    size_z = jnp.clip(jnp.exp(jax.random.uniform(arg_keys[4], (EZ,), jnp.float32, math.log(0.5), math.log(2.0))), 0.5, 2.0)
    return dict(element_load=element_load, orient=orient, size_x=size_x, size_y=size_y, size_z=size_z)


precise = lax.Precision.HIGHEST

def legendre_pair(value):
    prev_val = 1.0
    curr_val = value
    prev_der = 0.0
    curr_der = 1.0
    for order in range(2, 8):
        next_val = ((2 * order - 1) * value * curr_val - (order - 1) * prev_val) / order
        next_der = prev_der + (2 * order - 1) * curr_val
        prev_val, curr_val = (curr_val, next_val)
        prev_der, curr_der = (curr_der, next_der)
    return (curr_val, curr_der)

def second_derivative(value):
    leg_val, leg_der = legendre_pair(value)
    return (2.0 * value * leg_der - 56.0 * leg_val) / (1.0 - value * value)

def basis_tables():
    guesses = [-0.8717401485096066, -0.5917001814331423, -0.2092992179024789, 0.2092992179024789, 0.5917001814331423, 0.8717401485096066]
    inner_pts = []
    for guess in guesses:
        point = guess
        for newton in range(4):
            point = point - legendre_pair(point)[1] / second_derivative(point)
        inner_pts.append(point)
    gll_points = [-1.0] + inner_pts + [1.0]
    leg_values = [legendre_pair(point)[0] for point in gll_points]
    weights = [2.0 / (56.0 * lv * lv) for lv in leg_values]
    derivative = [[0.0] * 8 for row_at in range(8)]
    for row_at in range(8):
        for col_at in range(8):
            if row_at != col_at:
                derivative[row_at][col_at] = leg_values[row_at] / (leg_values[col_at] * (gll_points[row_at] - gll_points[col_at]))
    derivative[0][0] = -14.0
    derivative[7][7] = 14.0
    stiffness = [[sum((derivative[mid][row_at] * weights[mid] * derivative[mid][col_at] for mid in range(8))) for col_at in range(8)] for row_at in range(8)]
    inv_sqrt = [1.0 / math.sqrt(wt) for wt in weights]
    matrix = [[inv_sqrt[row_at] * stiffness[row_at][col_at] * inv_sqrt[col_at] for col_at in range(8)] for row_at in range(8)]
    vectors = [[1.0 if row_at == col_at else 0.0 for col_at in range(8)] for row_at in range(8)]
    for sweep in range(14):
        for first in range(8):
            for second in range(first + 1, 8):
                angle = 0.5 * math.atan2(2.0 * matrix[first][second], matrix[second][second] - matrix[first][first])
                cosine = math.cos(angle)
                sine = math.sin(angle)
                for other in range(8):
                    left_val = matrix[other][first]
                    right_val = matrix[other][second]
                    matrix[other][first] = cosine * left_val - sine * right_val
                    matrix[other][second] = sine * left_val + cosine * right_val
                for other in range(8):
                    left_val = matrix[first][other]
                    right_val = matrix[second][other]
                    matrix[first][other] = cosine * left_val - sine * right_val
                    matrix[second][other] = sine * left_val + cosine * right_val
                for other in range(8):
                    left_val = vectors[other][first]
                    right_val = vectors[other][second]
                    vectors[other][first] = cosine * left_val - sine * right_val
                    vectors[other][second] = sine * left_val + cosine * right_val
    eigen_vals = [max(matrix[idx_at][idx_at], 0.0) for idx_at in range(8)]
    eigen_modes = [[inv_sqrt[row_at] * vectors[row_at][col_at] for col_at in range(8)] for row_at in range(8)]
    return (jnp.asarray(weights, jnp.float32), jnp.asarray(stiffness, jnp.float32), jnp.asarray(eigen_modes, jnp.float32), jnp.asarray(eigen_vals, jnp.float32))

def on_points(cube):
    return cube[None, None, :, :, :, None]

def flip_frame(field_in, orient):
    for bit_at in range(3):
        flipped = (orient // 2 ** bit_at % 2 == 1)[:, :, None, None, None, :]
        field_in = jnp.where(flipped, jnp.flip(field_in, axis=2 + bit_at), field_in)
    return field_in

def face_weights(global_index, total_count):
    lower_face = jnp.where(global_index == 0, 0.0, 0.5).astype(jnp.float32)
    upper_face = jnp.where(global_index == total_count - 1, 0.0, 0.5).astype(jnp.float32)
    middle = jnp.ones((6, global_index.shape[0]), jnp.float32)
    return jnp.concatenate([lower_face[None], middle, upper_face[None]], axis=0)

def point_weights(weight_x, weight_y, weight_z):
    return weight_x.T[:, None, :, None, None, None] * weight_y.T[None, :, None, :, None, None] * weight_z[None, None, None, None, :, :]

def coefficients(size_x, size_y, size_z, eigen_vals):
    coef_x = (size_y[None, :, None] * size_z[None, None, :] / (2.0 * size_x[:, None, None]))[:, :, None, None, None, :]
    coef_y = (size_x[:, None, None] * size_z[None, None, :] / (2.0 * size_y[None, :, None]))[:, :, None, None, None, :]
    coef_z = (size_x[:, None, None] * size_y[None, :, None] / (2.0 * size_z[None, None, :]))[:, :, None, None, None, :]
    denominator = on_points(eigen_vals[:, None, None]) * coef_x + on_points(eigen_vals[None, :, None]) * coef_y + on_points(eigen_vals[None, None, :]) * coef_z + (coef_x + coef_y + coef_z) / 3.0
    return (coef_x, coef_y, coef_z, denominator)

def along(matrix, field_in, axis_at):
    einsum_forms = ['ai,xyijkz->xyajkz', 'aj,xyijkz->xyiakz', 'ak,xyijkz->xyijaz']
    return jnp.einsum(einsum_forms[axis_at], matrix, field_in, precision=precise)

def laplace(field_in, tables, coefs):
    weights, stiffness = (tables[0], tables[1])
    w_first = weights[:, None, None]
    w_second = weights[None, :, None]
    w_third = weights[None, None, :]
    term_x = along(stiffness, field_in, 0) * on_points(w_second * w_third) * coefs[0]
    term_y = along(stiffness, field_in, 1) * on_points(w_first * w_third) * coefs[1]
    term_z = along(stiffness, field_in, 2) * on_points(w_first * w_second) * coefs[2]
    return term_x + term_y + term_z

def element_solve(field_in, tables, coefs):
    eigen_modes = tables[2]
    spectral = along(eigen_modes.T, along(eigen_modes.T, along(eigen_modes.T, field_in, 0), 1), 2)
    spectral = spectral / coefs[3]
    return along(eigen_modes, along(eigen_modes, along(eigen_modes, spectral, 0), 1), 2)

def face_pair(field_in, dim_at):
    point_dim = 2 + dim_at
    lower_face = lax.index_in_dim(field_in, 0, point_dim, keepdims=False)
    upper_face = lax.index_in_dim(field_in, 7, point_dim, keepdims=False)
    return (lower_face, upper_face)

def assemble(field_in, dim_at, lower_face, upper_face, from_next, from_prev):
    point_dim = 2 + dim_at
    elem_dim = [0, 1, 4][dim_at]
    elements = lower_face.shape[elem_dim]
    after_face = jnp.concatenate([lax.slice_in_dim(lower_face, 1, elements, axis=elem_dim), from_next], axis=elem_dim)
    before = jnp.concatenate([from_prev, lax.slice_in_dim(upper_face, 0, elements - 1, axis=elem_dim)], axis=elem_dim)
    middle = lax.slice_in_dim(field_in, 1, 7, axis=point_dim)
    return jnp.concatenate([jnp.expand_dims(lower_face + before, point_dim), middle, jnp.expand_dims(upper_face + after_face, point_dim)], axis=point_dim)

def summed(field_in):
    for dim_at in range(3):
        elem_dim = [0, 1, 4][dim_at]
        lower_face, upper_face = face_pair(field_in, dim_at)
        zero_slab = jnp.zeros_like(lax.slice_in_dim(lower_face, 0, 1, axis=elem_dim))
        field_in = assemble(field_in, dim_at, lower_face, upper_face, zero_slab, zero_slab)
    return field_in

def reference(element_load, orient, size_x, size_y, size_z):
    tables = basis_tables()
    weight = point_weights(face_weights(jnp.arange(EXG, dtype=jnp.int32), EXG), face_weights(jnp.arange(EYG, dtype=jnp.int32), EYG), face_weights(jnp.arange(EZ, dtype=jnp.int32), EZ))
    interior = (weight > 0.0).astype(jnp.float32)
    coefs = coefficients(size_x, size_y, size_z, tables[3])

    def operator(field_in):
        return interior * summed(laplace(field_in, tables, coefs))

    def precondition(field_in):
        return interior * summed(element_solve(field_in, tables, coefs))

    def inner_product(left_field, right_field):
        return jnp.sum(left_field * right_field * weight)
    right_side = interior * summed(flip_frame(element_load, orient))
    solution = jnp.zeros_like(right_side)
    residual = right_side
    precond = precondition(residual)
    direction = precond
    energy_old = inner_product(residual, precond)
    for step_at in range(ITERS):
        applied = operator(direction)
        step_len = energy_old / inner_product(direction, applied)
        solution = solution + step_len * direction
        residual = residual - step_len * applied
        if step_at + 1 < ITERS:
            precond = precondition(residual)
            energy_new = inner_product(residual, precond)
            direction = precond + energy_new / energy_old * direction
            energy_old = energy_new
    return (flip_frame(solution, orient), flip_frame(residual, orient))
```

```python
import math

import jax
import jax.numpy as jnp
from jax import lax
from jax.sharding import PartitionSpec as P

ITERS = 2


precise = lax.Precision.HIGHEST


def passed_along(x, axis, by):
    peers = lax.axis_size(axis)
    pairs = [(i, i + by) for i in range(peers) if 0 <= i + by < peers]
    return lax.ppermute(x, axis, pairs)


def legendre_pair(value):
    prev_val = 1.0
    curr_val = value
    prev_der = 0.0
    curr_der = 1.0
    for order in range(2, 8):
        next_val = ((2 * order - 1) * value * curr_val - (order - 1) * prev_val) / order
        next_der = prev_der + (2 * order - 1) * curr_val
        prev_val, curr_val = (curr_val, next_val)
        prev_der, curr_der = (curr_der, next_der)
    return (curr_val, curr_der)


def second_derivative(value):
    leg_val, leg_der = legendre_pair(value)
    return (2.0 * value * leg_der - 56.0 * leg_val) / (1.0 - value * value)


def basis_tables():
    guesses = [
        -0.8717401485096066,
        -0.5917001814331423,
        -0.2092992179024789,
        0.2092992179024789,
        0.5917001814331423,
        0.8717401485096066,
    ]
    inner_pts = []
    for guess in guesses:
        point = guess
        for newton in range(4):
            point = point - legendre_pair(point)[1] / second_derivative(point)
        inner_pts.append(point)
    gll_points = [-1.0] + inner_pts + [1.0]
    leg_values = [legendre_pair(point)[0] for point in gll_points]
    weights = [2.0 / (56.0 * lv * lv) for lv in leg_values]
    derivative = [[0.0] * 8 for row_at in range(8)]
    for row_at in range(8):
        for col_at in range(8):
            if row_at != col_at:
                derivative[row_at][col_at] = leg_values[row_at] / (
                    leg_values[col_at] * (gll_points[row_at] - gll_points[col_at])
                )
    derivative[0][0] = -14.0
    derivative[7][7] = 14.0
    stiffness = [
        [
            sum(
                (
                    derivative[mid][row_at] * weights[mid] * derivative[mid][col_at]
                    for mid in range(8)
                )
            )
            for col_at in range(8)
        ]
        for row_at in range(8)
    ]
    inv_sqrt = [1.0 / math.sqrt(wt) for wt in weights]
    matrix = [
        [inv_sqrt[row_at] * stiffness[row_at][col_at] * inv_sqrt[col_at] for col_at in range(8)]
        for row_at in range(8)
    ]
    vectors = [[1.0 if row_at == col_at else 0.0 for col_at in range(8)] for row_at in range(8)]
    for sweep in range(14):
        for first in range(8):
            for second in range(first + 1, 8):
                angle = 0.5 * math.atan2(
                    2.0 * matrix[first][second], matrix[second][second] - matrix[first][first]
                )
                cosine = math.cos(angle)
                sine = math.sin(angle)
                for other in range(8):
                    left_val = matrix[other][first]
                    right_val = matrix[other][second]
                    matrix[other][first] = cosine * left_val - sine * right_val
                    matrix[other][second] = sine * left_val + cosine * right_val
                for other in range(8):
                    left_val = matrix[first][other]
                    right_val = matrix[second][other]
                    matrix[first][other] = cosine * left_val - sine * right_val
                    matrix[second][other] = sine * left_val + cosine * right_val
                for other in range(8):
                    left_val = vectors[other][first]
                    right_val = vectors[other][second]
                    vectors[other][first] = cosine * left_val - sine * right_val
                    vectors[other][second] = sine * left_val + cosine * right_val
    eigen_vals = [max(matrix[idx_at][idx_at], 0.0) for idx_at in range(8)]
    eigen_modes = [
        [inv_sqrt[row_at] * vectors[row_at][col_at] for col_at in range(8)] for row_at in range(8)
    ]
    return (
        jnp.asarray(weights, jnp.float32),
        jnp.asarray(stiffness, jnp.float32),
        jnp.asarray(eigen_modes, jnp.float32),
        jnp.asarray(eigen_vals, jnp.float32),
    )


def on_points(cube):
    return cube[None, None, :, :, :, None]


def flip_frame(field_in, orient):
    for bit_at in range(3):
        flipped = (orient // 2**bit_at % 2 == 1)[:, :, None, None, None, :]
        field_in = jnp.where(flipped, jnp.flip(field_in, axis=2 + bit_at), field_in)
    return field_in


def face_weights(global_index, total_count):
    lower_face = jnp.where(global_index == 0, 0.0, 0.5).astype(jnp.float32)
    upper_face = jnp.where(global_index == total_count - 1, 0.0, 0.5).astype(jnp.float32)
    middle = jnp.ones((6, global_index.shape[0]), jnp.float32)
    return jnp.concatenate([lower_face[None], middle, upper_face[None]], axis=0)


def point_weights(weight_x, weight_y, weight_z):
    return (
        weight_x.T[:, None, :, None, None, None]
        * weight_y.T[None, :, None, :, None, None]
        * weight_z[None, None, None, None, :, :]
    )


def coefficients(size_x, size_y, size_z, eigen_vals):
    coef_x = (size_y[None, :, None] * size_z[None, None, :] / (2.0 * size_x[:, None, None]))[
        :, :, None, None, None, :
    ]
    coef_y = (size_x[:, None, None] * size_z[None, None, :] / (2.0 * size_y[None, :, None]))[
        :, :, None, None, None, :
    ]
    coef_z = (size_x[:, None, None] * size_y[None, :, None] / (2.0 * size_z[None, None, :]))[
        :, :, None, None, None, :
    ]
    denominator = (
        on_points(eigen_vals[:, None, None]) * coef_x
        + on_points(eigen_vals[None, :, None]) * coef_y
        + on_points(eigen_vals[None, None, :]) * coef_z
        + (coef_x + coef_y + coef_z) / 3.0
    )
    return (coef_x, coef_y, coef_z, denominator)


def along(matrix, field_in, axis_at):
    einsum_forms = ["ai,xyijkz->xyajkz", "aj,xyijkz->xyiakz", "ak,xyijkz->xyijaz"]
    return jnp.einsum(einsum_forms[axis_at], matrix, field_in, precision=precise)


def laplace(field_in, tables, coefs):
    weights, stiffness = (tables[0], tables[1])
    w_first = weights[:, None, None]
    w_second = weights[None, :, None]
    w_third = weights[None, None, :]
    term_x = along(stiffness, field_in, 0) * on_points(w_second * w_third) * coefs[0]
    term_y = along(stiffness, field_in, 1) * on_points(w_first * w_third) * coefs[1]
    term_z = along(stiffness, field_in, 2) * on_points(w_first * w_second) * coefs[2]
    return term_x + term_y + term_z


def element_solve(field_in, tables, coefs):
    eigen_modes = tables[2]
    spectral = along(eigen_modes.T, along(eigen_modes.T, along(eigen_modes.T, field_in, 0), 1), 2)
    spectral = spectral / coefs[3]
    return along(eigen_modes, along(eigen_modes, along(eigen_modes, spectral, 0), 1), 2)


def face_pair(field_in, dim_at):
    point_dim = 2 + dim_at
    lower_face = lax.index_in_dim(field_in, 0, point_dim, keepdims=False)
    upper_face = lax.index_in_dim(field_in, 7, point_dim, keepdims=False)
    return (lower_face, upper_face)


def assemble(field_in, dim_at, lower_face, upper_face, from_next, from_prev):
    point_dim = 2 + dim_at
    elem_dim = [0, 1, 4][dim_at]
    elements = lower_face.shape[elem_dim]
    after_face = jnp.concatenate(
        [lax.slice_in_dim(lower_face, 1, elements, axis=elem_dim), from_next], axis=elem_dim
    )
    before = jnp.concatenate(
        [from_prev, lax.slice_in_dim(upper_face, 0, elements - 1, axis=elem_dim)], axis=elem_dim
    )
    middle = lax.slice_in_dim(field_in, 1, 7, axis=point_dim)
    return jnp.concatenate(
        [
            jnp.expand_dims(lower_face + before, point_dim),
            middle,
            jnp.expand_dims(upper_face + after_face, point_dim),
        ],
        axis=point_dim,
    )


def remote_x(lower_face, upper_face):
    elements = lower_face.shape[0]
    from_next = passed_along(lax.slice_in_dim(lower_face, 0, 1, axis=0), "node", -1)
    from_prev = passed_along(
        lax.slice_in_dim(upper_face, elements - 1, elements, axis=0), "node", 1
    )
    return (from_next, from_prev)


def remote_y(lower_face, upper_face):
    from_next = passed_along(lower_face, "dev", -1)
    from_prev = passed_along(upper_face, "dev", 1)
    return (from_next, from_prev)


def summed(field_in):
    lower_face, upper_face = face_pair(field_in, 0)
    from_next, from_prev = remote_x(lower_face, upper_face)
    field_in = assemble(field_in, 0, lower_face, upper_face, from_next, from_prev)
    lower_face, upper_face = face_pair(field_in, 1)
    from_next, from_prev = remote_y(lower_face, upper_face)
    field_in = assemble(field_in, 1, lower_face, upper_face, from_next, from_prev)
    lower_face, upper_face = face_pair(field_in, 2)
    zero_slab = jnp.zeros_like(lax.slice_in_dim(lower_face, 0, 1, axis=4))
    return assemble(field_in, 2, lower_face, upper_face, zero_slab, zero_slab)


def shards(element_load, orient, size_x, size_y, size_z):
    tables = basis_tables()
    count_x = element_load.shape[0]
    count_y = element_load.shape[1]
    count_z = element_load.shape[5]
    index_x = lax.axis_index("node") * count_x + jnp.arange(count_x, dtype=jnp.int32)
    index_y = lax.axis_index("dev") * count_y + jnp.arange(count_y, dtype=jnp.int32)
    weight = point_weights(
        face_weights(index_x, count_x * lax.axis_size("node")),
        face_weights(index_y, count_y * lax.axis_size("dev")),
        face_weights(jnp.arange(count_z, dtype=jnp.int32), count_z),
    )
    interior = (weight > 0.0).astype(jnp.float32)
    coefs = coefficients(size_x, size_y, size_z, tables[3])

    def apply(local):
        return interior * summed(local)

    load = apply(flip_frame(element_load, orient))
    local = element_solve(load, tables, coefs)
    dot_a = jnp.sum(load * local)
    first = apply(local)
    local = laplace(first, tables, coefs)
    dot_c = jnp.sum(first * local)
    image = apply(local)
    local = element_solve(image, tables, coefs)
    dot_d = jnp.sum(image * local)
    second = apply(local)
    local = laplace(second, tables, coefs)
    dot_e = jnp.sum(second * local)
    second_image = apply(local)
    sums = total(jnp.stack([dot_a, dot_c, dot_d, dot_e]))
    dot_a, dot_c, dot_d, dot_e = sums[0], sums[1], sums[2], sums[3]
    alpha = dot_a / dot_c
    energy = dot_a - 2.0 * alpha * dot_c + alpha * alpha * dot_d
    keep = 1.0 + energy / dot_a
    curve = keep * keep * dot_c - 2.0 * alpha * keep * dot_d + alpha * alpha * dot_e
    step = energy / curve
    answer = (alpha + step * keep) * first - (step * alpha) * second
    rest = load - (alpha + step * keep) * image + (step * alpha) * second_image
    return (flip_frame(answer, orient), flip_frame(rest, orient))


def total(values):
    row = jnp.zeros((1, 1, 128), jnp.float32).at[0, 0, :4].set(values)
    for axis in ("dev", "node"):
        sent = jnp.broadcast_to(row, (lax.axis_size(axis), 1, 128))
        row = jnp.sum(lax.all_to_all(sent, axis, 0, 0), axis=0, keepdims=True)
    return row[0, 0, :4]


def solution(mesh):
    return jax.shard_map(
        shards,
        mesh=mesh,
        in_specs=(
            P("node", "dev", None, None, None, None),
            P("node", "dev", None),
            P("node"),
            P("dev"),
            P(),
        ),
        out_specs=(
            P("node", "dev", None, None, None, None),
            P("node", "dev", None, None, None, None),
        ),
        check_vma=False,
    )
```

```python
import functools
import math

import jax
import jax.numpy as jnp
import ml_dtypes
import numpy as np
from jax import lax
from jax.experimental import pallas as pl
from jax.experimental.pallas import tpu as pltpu
from jax.sharding import PartitionSpec as P

F32 = jnp.float32
BF16 = jnp.bfloat16


def passed_along(x, axis, by):
    peers = lax.axis_size(axis)
    return lax.ppermute(x, axis, [(i, (i + by) % peers) for i in range(peers)])


def legendre_pair(value):
    prev_val = 1.0
    curr_val = value
    prev_der = 0.0
    curr_der = 1.0
    for order in range(2, 8):
        next_val = ((2 * order - 1) * value * curr_val - (order - 1) * prev_val) / order
        next_der = prev_der + (2 * order - 1) * curr_val
        prev_val, curr_val = (curr_val, next_val)
        prev_der, curr_der = (curr_der, next_der)
    return (curr_val, curr_der)


def second_derivative(value):
    leg_val, leg_der = legendre_pair(value)
    return (2.0 * value * leg_der - 56.0 * leg_val) / (1.0 - value * value)


def basis_tables():
    guesses = [
        -0.8717401485096066,
        -0.5917001814331423,
        -0.2092992179024789,
        0.2092992179024789,
        0.5917001814331423,
        0.8717401485096066,
    ]
    inner_pts = []
    for guess in guesses:
        point = guess
        for newton in range(4):
            point = point - legendre_pair(point)[1] / second_derivative(point)
        inner_pts.append(point)
    gll_points = [-1.0] + inner_pts + [1.0]
    leg_values = [legendre_pair(point)[0] for point in gll_points]
    weights = [2.0 / (56.0 * lv * lv) for lv in leg_values]
    derivative = [[0.0] * 8 for row_at in range(8)]
    for row_at in range(8):
        for col_at in range(8):
            if row_at != col_at:
                derivative[row_at][col_at] = leg_values[row_at] / (
                    leg_values[col_at] * (gll_points[row_at] - gll_points[col_at])
                )
    derivative[0][0] = -14.0
    derivative[7][7] = 14.0
    stiffness = [
        [
            sum(
                (
                    derivative[mid][row_at] * weights[mid] * derivative[mid][col_at]
                    for mid in range(8)
                )
            )
            for col_at in range(8)
        ]
        for row_at in range(8)
    ]
    inv_sqrt = [1.0 / math.sqrt(wt) for wt in weights]
    matrix = [
        [inv_sqrt[row_at] * stiffness[row_at][col_at] * inv_sqrt[col_at] for col_at in range(8)]
        for row_at in range(8)
    ]
    vectors = [[1.0 if row_at == col_at else 0.0 for col_at in range(8)] for row_at in range(8)]
    for sweep in range(14):
        for first in range(8):
            for second in range(first + 1, 8):
                angle = 0.5 * math.atan2(
                    2.0 * matrix[first][second], matrix[second][second] - matrix[first][first]
                )
                cosine = math.cos(angle)
                sine = math.sin(angle)
                for other in range(8):
                    left_val = matrix[other][first]
                    right_val = matrix[other][second]
                    matrix[other][first] = cosine * left_val - sine * right_val
                    matrix[other][second] = sine * left_val + cosine * right_val
                for other in range(8):
                    left_val = matrix[first][other]
                    right_val = matrix[second][other]
                    matrix[first][other] = cosine * left_val - sine * right_val
                    matrix[second][other] = sine * left_val + cosine * right_val
                for other in range(8):
                    left_val = vectors[other][first]
                    right_val = vectors[other][second]
                    vectors[other][first] = cosine * left_val - sine * right_val
                    vectors[other][second] = sine * left_val + cosine * right_val
    eigen_vals = [max(matrix[idx_at][idx_at], 0.0) for idx_at in range(8)]
    eigen_modes = [
        [inv_sqrt[row_at] * vectors[row_at][col_at] for col_at in range(8)] for row_at in range(8)
    ]
    return (weights, stiffness, eigen_modes, eigen_vals)


WEIGHTS, STIFF, MODES, LAMS = basis_tables()
EVEN = [MODES[0][m] * MODES[7][m] > 0 for m in range(8)]


def split_table(table):
    high = table.astype(ml_dtypes.bfloat16)
    low = (table - high.astype(np.float64)).astype(ml_dtypes.bfloat16)
    return [high, low]


def plane_tables():
    modes, stiff, weights = np.array(MODES), np.array(STIFF), np.diag(WEIGHTS)
    four = np.eye(4)
    forward = np.kron(four, np.kron(modes.T, modes.T))
    backward = np.kron(four, np.kron(modes, modes))
    along_j = np.kron(four, np.kron(stiff, weights))
    along_k = np.kron(four, np.kron(weights, stiff))
    solve = np.stack(split_table(forward) + split_table(backward))
    local = np.stack(split_table(along_j) + split_table(along_k))
    return solve, local


def rows(i, j):
    return slice((i * 8 + j) * 8, (i * 8 + j) * 8 + 8)


def plane(n):
    return slice(n * 64, n * 64 + 64)


def eight(n):
    return slice(n * 8, n * 8 + 8)


def lanes(x):
    return slice(x * 128, x * 128 + 128)


def weighted(values, factors):
    total = None
    for value, factor in zip(values, factors):
        term = value * factor
        total = term if total is None else total + term
    return total


def halves(v):
    return [v[a] + v[7 - a] for a in range(4)], [v[a] - v[7 - a] for a in range(4)]


def to_modes(v):
    even, odd = halves(v)
    return [weighted(even if EVEN[m] else odd, [MODES[a][m] for a in range(4)]) for m in range(8)]


def from_modes(t):
    out = [None] * 8
    for a in range(4):
        even = weighted([t[m] for m in range(8) if EVEN[m]], [MODES[a][m] for m in range(8) if EVEN[m]])
        odd = weighted([t[m] for m in range(8) if not EVEN[m]], [MODES[a][m] for m in range(8) if not EVEN[m]])
        out[a], out[7 - a] = even + odd, even - odd
    return out


def stiff_line(v):
    even, odd = halves(v)
    out = [None] * 8
    for i in range(4):
        first = weighted(even, [0.5 * (STIFF[i][a] + STIFF[i][7 - a]) for a in range(4)])
        second = weighted(odd, [0.5 * (STIFF[i][a] - STIFF[i][7 - a]) for a in range(4)])
        out[i], out[7 - i] = first + second, first - second
    return out


def store_split(high_ref, low_ref, row, column, parts):
    chunk = jnp.concatenate(parts, axis=0)
    high = chunk.astype(BF16)
    low = (chunk - high.astype(F32)).astype(BF16)
    high_ref[row : row + 16, column] = high
    low_ref[row : row + 16, column] = low


def product(table, at, high, low):
    dot = functools.partial(jnp.dot, preferred_element_type=F32)
    return dot(table[at], high) + dot(table[at], low) + dot(table[at + 1], high)


def z_summed(ref):
    lane = lax.broadcasted_iota(jnp.int32, (8, 128), 1)
    for x in range(2):
        for i in range(8):
            first = ref[x, pl.ds(i * 64, 8, stride=8), :]
            last = ref[x, pl.ds(i * 64 + 7, 8, stride=8), :]
            ref[x, pl.ds(i * 64, 8, stride=8), :] = jnp.where(lane == 0, 0.0, first + pltpu.roll(last, 1, 1))
            ref[x, pl.ds(i * 64 + 7, 8, stride=8), :] = jnp.where(lane == 127, 0.0, last + pltpu.roll(first, 127, 1))


def x_joined(ref):
    both = ref[0, plane(7), :] + ref[1, plane(0), :]
    ref[0, plane(7), :] = both
    ref[1, plane(0), :] = both


def y_faces(ref, low_ref, high_ref):
    for x in range(2):
        for i in range(8):
            low_ref[x, eight(i), :] = ref[x, rows(i, 0), :]
            high_ref[x, eight(i), :] = ref[x, rows(i, 7), :]


def y_joined(value, x, i, j, before, after, coef):
    if j == 0:
        value = (value + before[x, eight(i), :]) * coef[0, 4]
    if j == 7:
        value = (value + after[x, eight(i), :]) * coef[1, 4]
    return value


def sublane_table(values):
    at = lax.broadcasted_iota(jnp.int32, (8, 128), 0)
    out = jnp.full((8, 128), values[7], F32)
    for n in range(7):
        out = jnp.where(at == n, values[n], out)
    return out


def over_sublanes(row):
    return jnp.broadcast_to(row, (8, 128))


def reversed_points(src, mid, out, orient):
    for x in range(2):
        code = over_sublanes(orient[x : x + 1, :])
        flip_i, flip_j, flip_k = (code & 1) != 0, (code & 2) != 0, (code & 4) != 0
        for i in range(4):
            for j in range(4):
                a, b = src[x, rows(i, j), :], src[x, rows(7 - i, j), :]
                c, d = src[x, rows(i, 7 - j), :], src[x, rows(7 - i, 7 - j), :]
                a, b = jnp.where(flip_i, b, a), jnp.where(flip_i, a, b)
                c, d = jnp.where(flip_i, d, c), jnp.where(flip_i, c, d)
                mid[x, rows(i, j), :] = jnp.where(flip_j, c, a)
                mid[x, rows(i, 7 - j), :] = jnp.where(flip_j, a, c)
                mid[x, rows(7 - i, j), :] = jnp.where(flip_j, d, b)
                mid[x, rows(7 - i, 7 - j), :] = jnp.where(flip_j, b, d)
        for i in range(8):
            for k in range(4):
                a = mid[x, pl.ds(i * 64 + k, 8, stride=8), :]
                b = mid[x, pl.ds(i * 64 + 7 - k, 8, stride=8), :]
                out[x, pl.ds(i * 64 + k, 8, stride=8), :] = jnp.where(flip_k, b, a)
                out[x, pl.ds(i * 64 + 7 - k, 8, stride=8), :] = jnp.where(flip_k, a, b)


def start_kernel(numbers, load, orient, size_z, field, y_low, y_high, x_low, x_high, coef, mid):
    reversed_points(load, mid, field, orient)
    z_summed(field)
    x_joined(field)
    y_faces(field, y_low, y_high)
    size_y = numbers[2]
    length = over_sublanes(size_z[...])
    weight_k = sublane_table(WEIGHTS)
    lam_k = sublane_table(LAMS)
    at = lax.broadcasted_iota(jnp.int32, (8, 128), 0)
    for x in range(2):
        size_x = numbers[x]
        coef_x = size_y * length / (2.0 * jnp.full((8, 128), size_x, F32))
        coef_y = size_x * length / (2.0 * jnp.full((8, 128), size_y, F32))
        coef_z = jnp.full((8, 128), size_x * size_y, F32) / (2.0 * length)
        coef[x, 0] = jnp.where(at == 0, coef_x, jnp.where(at == 1, coef_y, coef_z))
        coef[x, 1] = coef_x * weight_k
        coef[x, 2] = lam_k * coef_z + (coef_x + coef_y + coef_z) / 3.0
        coef[x, 3] = jnp.full((8, 128), numbers[3 + x], F32)
        coef[x, 4] = jnp.full((8, 128), numbers[5 + x], F32)
        coef[x, 5] = weight_k
    x_low[0:64, :] = field[0, plane(0), :]
    x_high[0:64, :] = field[1, plane(7), :]
    x_low[64:72, :] = coef[0, 0]
    x_high[64:72, :] = coef[1, 0]


def edge_kernel(x_low, x_high, before, after, low_out, high_out):
    low_out[...] = x_low[...]
    high_out[...] = x_high[...]
    low_out[0:8, :] += before[0, 0:8, :]
    low_out[56:64, :] += after[0, 0:8, :]
    high_out[0:8, :] += before[1, 56:64, :]
    high_out[56:64, :] += after[1, 56:64, :]


def solve_kernel(with_x, *refs):
    coef, table, field, before, after = refs[:5]
    refs = refs[5:]
    if with_x:
        x_before, x_after = refs[:2]
        refs = refs[2:]
    joined, out, y_low, y_high, dot, high, low, mid = refs
    for x in range(2):
        for pair in range(4):
            lines = []
            for j in (2 * pair, 2 * pair + 1):
                line = []
                for i in range(8):
                    value = y_joined(field[x, rows(i, j), :], x, i, j, before, after, coef)
                    if with_x and x == 0 and i == 0:
                        value = (value + x_before[eight(j), :]) * coef[0, 3] * (
                            coef[0, 4] if j == 0 else coef[1, 4] if j == 7 else 1.0
                        )
                    if with_x and x == 1 and i == 7:
                        value = (value + x_after[eight(j), :]) * coef[1, 3] * (
                            coef[0, 4] if j == 0 else coef[1, 4] if j == 7 else 1.0
                        )
                    joined[x, rows(i, j), :] = value
                    line.append(value)
                lines.append(to_modes(line))
            for m in range(8):
                store_split(high, low, m * 64 + pair * 16, lanes(x), [lines[0][m], lines[1][m]])
    for block in range(2):
        part = slice(block * 256, block * 256 + 256)
        mid[part, :] = product(table, 0, high[part, :], low[part, :])
    for x in range(2):
        coef_x, coef_y = over_sublanes(coef[x, 0, 0:1, :]), over_sublanes(coef[x, 0, 1:2, :])
        den_i = [coef_x * LAMS[m] for m in range(8)]
        den_j = [coef_y * LAMS[n] + coef[x, 2] for n in range(8)]
        for m in range(8):
            for pair in range(4):
                parts = [mid[rows(m, n), lanes(x)] / (den_i[m] + den_j[n]) for n in (2 * pair, 2 * pair + 1)]
                store_split(high, low, m * 64 + pair * 16, lanes(x), parts)
    for block in range(2):
        part = slice(block * 256, block * 256 + 256)
        mid[part, :] = product(table, 2, high[part, :], low[part, :])
    total = jnp.zeros((8, 128), F32)
    for x in range(2):
        for j in range(8):
            line = from_modes([mid[rows(m, j), lanes(x)] for m in range(8)])
            for i in range(8):
                out[x, rows(i, j), :] = line[i]
                total = total + line[i] * joined[x, rows(i, j), :]
    dot[...] = total
    z_summed(out)
    x_joined(out)
    y_faces(out, y_low, y_high)


def local_kernel(coef, table, field, before, after, joined, out, x_low, x_high, high, low, first, second):
    for x in range(2):
        for pair in range(4):
            for i in range(8):
                parts = []
                for j in (2 * pair, 2 * pair + 1):
                    value = y_joined(field[x, rows(i, j), :], x, i, j, before, after, coef)
                    if x == 0 and i == 0:
                        value = value * coef[0, 3]
                    if x == 1 and i == 7:
                        value = value * coef[1, 3]
                    joined[x, rows(i, j), :] = value
                    parts.append(value)
                store_split(high, low, i * 64 + pair * 16, lanes(x), parts)
    for block in range(2):
        part = slice(block * 256, block * 256 + 256)
        first[part, :] = product(table, 0, high[part, :], low[part, :])
        second[part, :] = product(table, 2, high[part, :], low[part, :])
    for x in range(2):
        coef_y, coef_z = over_sublanes(coef[x, 0, 1:2, :]), over_sublanes(coef[x, 0, 2:3, :])
        for j in range(8):
            scale = coef[x, 1] * WEIGHTS[j]
            line = stiff_line([joined[x, rows(i, j), :] for i in range(8)])
            for i in range(8):
                flat = coef_y * first[rows(i, j), lanes(x)] + coef_z * second[rows(i, j), lanes(x)]
                out[x, rows(i, j), :] = scale * line[i] + WEIGHTS[i] * flat
    x_low[0:64, :] = joined[0, plane(0), :]
    x_low[64:128, :] = out[0, plane(0), :]
    x_high[0:64, :] = joined[1, plane(7), :]
    x_high[64:128, :] = out[1, plane(7), :]


def cross_kernel(with_row, *refs):
    coef, table, field, local, x_before, x_after, kind_before, kind_after = refs[:8]
    refs = refs[8:]
    if with_row:
        earlier = refs[:3]
        refs = refs[3:]
    joined, out, y_low, y_high, dot, high, low, first, second = refs
    joined[...] = field[...]
    for pair in range(4):
        parts = [[], [], [], []]
        for j in (2 * pair, 2 * pair + 1):
            for side in range(2):
                own = field[side, rows(7 * side, j), :]
                came = (x_after if side else x_before)[eight(j), :] * coef[side, 3]
                joined[side, rows(7 * side, j), :] = own + came
                parts[side].append(came)
                parts[2 + side].append(own)
        for n in range(4):
            store_split(high, low, n * 64 + pair * 16, slice(0, 128), parts[n])
    first[...] = product(table, 0, high[...], low[...])
    second[...] = product(table, 2, high[...], low[...])
    total = jnp.zeros((8, 128), F32)
    for side in range(2):
        end = 7 * side
        coef_y, coef_z = over_sublanes(coef[side, 0, 1:2, :]), over_sublanes(coef[side, 0, 2:3, :])
        kind, sent = (kind_after, x_after) if side else (kind_before, x_before)
        far_x, far_y, far_z = [over_sublanes(kind[64 + n : 65 + n, :]) for n in range(3)]
        for j in range(8):
            came = sent[eight(j), :] * coef[side, 3]
            own = field[side, rows(end, j), :]
            pulled = coef[side, 1] * WEIGHTS[j] * came
            for i in range(8):
                value = local[side, rows(i, j), :] + STIFF[i][end] * pulled
                if i == end:
                    flat = coef_y * first[rows(side, j), :] + coef_z * second[rows(side, j), :]
                    value = value + WEIGHTS[end] * flat
                total = total + value * joined[side, rows(i, j), :]
                if i == end:
                    far = sent[64 + j * 8 : 72 + j * 8, :]
                    far = far + (STIFF[7 - end][7 - end] * WEIGHTS[j]) * (far_x * coef[side, 5]) * own
                    flat = far_y * first[rows(2 + side, j), :] + far_z * second[rows(2 + side, j), :]
                    far = far + WEIGHTS[7 - end] * flat
                    value = (value + far) * coef[side, 3]
                out[side, rows(i, j), :] = value
    z_summed(out)
    x_joined(out)
    y_faces(out, y_low, y_high)
    if with_row:
        lane = lax.broadcasted_iota(jnp.int32, (64, 128), 1)
        row = jnp.zeros((64, 128), F32)
        for n, value in enumerate([ref[...] for ref in earlier] + [total]):
            row = jnp.where(lane == n, jnp.sum(value), row)
        dot[...] = row
    else:
        dot[...] = total


def sum_kernel(parts, out):
    out[...] = over_sublanes(jnp.sum(parts[...], axis=0, keepdims=True))


def end_kernel(coef, orient, sums, last, before, after, load, first, image, second, answer, rest, one, two):
    lane = lax.broadcasted_iota(jnp.int32, (8, 128), 1)
    dots = [jnp.full((8, 128), jnp.sum(jnp.where(lane == n, sums[...], 0.0)), F32) for n in range(4)]
    alpha = dots[0] / dots[1]
    energy = dots[0] - 2.0 * alpha * dots[1] + alpha * alpha * dots[2]
    keep = 1.0 + energy / dots[0]
    curve = keep * keep * dots[1] - 2.0 * alpha * keep * dots[2] + alpha * alpha * dots[3]
    step = energy / curve
    on_first = alpha + step * keep
    on_second = step * alpha
    for x in range(2):
        for i in range(8):
            for j in range(8):
                at = rows(i, j)
                value = y_joined(last[x, at, :], x, i, j, before, after, coef)
                one[x, at, :] = on_first * first[x, at, :] - on_second * second[x, at, :]
                two[x, at, :] = load[x, at, :] - on_first * image[x, at, :] + on_second * value
    reversed_points(one, one, answer, orient)
    reversed_points(two, two, rest, orient)


def f32(*shape):
    return jax.ShapeDtypeStruct(shape, F32)


def call(kernel, outs, scratch, *args, scalars=0):
    return pl.pallas_call(
        kernel,
        out_shape=outs,
        in_specs=[pl.BlockSpec(memory_space=pltpu.SMEM)] * scalars
        + [pl.BlockSpec(memory_space=pltpu.VMEM)] * (len(args) - scalars),
        out_specs=jax.tree.map(lambda _: pl.BlockSpec(memory_space=pltpu.VMEM), outs),
        scratch_shapes=scratch,
        compiler_params=pltpu.CompilerParams(vmem_limit_bytes=24 * 1024 * 1024),
    )(*args)


FIELD = f32(2, 512, 128)
FACES = [f32(2, 64, 128)] * 2
EIGHT = f32(8, 128)


def swap_y(low, high):
    return passed_along(high, "dev", 1), passed_along(low, "dev", -1)


def swap_x(low, high):
    return passed_along(high, "node", 1), passed_along(low, "node", -1)


def shards(element_load, orient, size_x, size_y, size_z):
    solve_np, local_np = plane_tables()
    solve_table, local_table = jnp.asarray(solve_np), jnp.asarray(local_np)
    node, dev = lax.axis_index("node"), lax.axis_index("dev")
    ends = jnp.stack(
        [node > 0, node < lax.axis_size("node") - 1, dev > 0, dev < lax.axis_size("dev") - 1]
    ).astype(F32)
    numbers = jnp.concatenate([size_x, size_y, ends, jnp.zeros((1,), F32)])
    orient = orient.reshape(2, 128)

    field, y_low, y_high, x_low, x_high, coef = call(
        start_kernel,
        [FIELD, *FACES, f32(72, 128), f32(72, 128), f32(2, 8, 8, 128)],
        [pltpu.VMEM((2, 512, 128), F32)],
        numbers, element_load.reshape(2, 512, 128), orient, size_z.reshape(1, 128),
        scalars=1,
    )
    y_came = swap_y(y_low, y_high)
    x_faces = call(edge_kernel, [f32(72, 128)] * 2, [], x_low, x_high, *y_came)
    kinds = swap_x(*x_faces)

    def solved(field, y_came, x_came):
        joined, out, low, high, dot = call(
            functools.partial(solve_kernel, bool(x_came)),
            [FIELD, FIELD, *FACES, EIGHT],
            [pltpu.VMEM((512, 256), BF16)] * 2 + [pltpu.VMEM((512, 256), F32)],
            coef, solve_table, field, *y_came, *x_came,
        )
        return joined, out, swap_y(low, high), dot

    def applied(field, y_came, earlier):
        joined, local, low, high = call(
            local_kernel,
            [FIELD, FIELD, f32(128, 128), f32(128, 128)],
            [pltpu.VMEM((512, 256), BF16)] * 2 + [pltpu.VMEM((512, 256), F32)] * 2,
            coef, local_table, field, *y_came,
        )
        x_came = swap_x(low, high)
        joined, out, low, high, dot = call(
            functools.partial(cross_kernel, bool(earlier)),
            [FIELD, FIELD, *FACES, f32(64, 128) if earlier else EIGHT],
            [pltpu.VMEM((256, 128), BF16)] * 2 + [pltpu.VMEM((256, 128), F32)] * 2,
            coef, local_table, joined, local, *x_came, *kinds, *earlier,
        )
        return joined, out, swap_y(low, high), dot

    load, out, y_came, dot_a = solved(field, y_came, kinds)
    first, out, y_came, dot_c = applied(out, y_came, ())
    image, out, y_came, dot_d = solved(out, y_came, ())
    second, out, y_came, row = applied(out, y_came, (dot_a, dot_c, dot_d))
    row = lax.all_to_all(row.reshape(64, 1, 128), "dev", 0, 0).reshape(64, 128)
    row = call(sum_kernel, EIGHT, [], row)
    row = lax.all_to_all(row.reshape(8, 1, 128), "node", 0, 0).reshape(8, 128)
    answer, rest = call(
        end_kernel,
        [FIELD, FIELD],
        [pltpu.VMEM((2, 512, 128), F32)] * 2,
        coef, orient, row, out, *y_came, load, first, image, second,
    )
    return answer.reshape(element_load.shape), rest.reshape(element_load.shape)


def solution(mesh):
    return jax.shard_map(
        shards,
        mesh=mesh,
        in_specs=(
            P("node", "dev", None, None, None, None),
            P("node", "dev", None),
            P("node"),
            P("dev"),
            P(),
        ),
        out_specs=(
            P("node", "dev", None, None, None, None),
            P("node", "dev", None, None, None, None),
        ),
        check_vma=False,
    )
```

```python
import functools
import math

import jax
import jax.numpy as jnp
import ml_dtypes
import numpy as np
from jax import lax
from jax.experimental import pallas as pl
from jax.experimental.pallas import tpu as pltpu
from jax.sharding import PartitionSpec as P

F32 = jnp.float32
BF16 = jnp.bfloat16


def passed_along(x, axis, by):
    peers = lax.axis_size(axis)
    return lax.ppermute(x, axis, [(i, (i + by) % peers) for i in range(peers)])


def legendre_pair(value):
    prev_val = 1.0
    curr_val = value
    prev_der = 0.0
    curr_der = 1.0
    for order in range(2, 8):
        next_val = ((2 * order - 1) * value * curr_val - (order - 1) * prev_val) / order
        next_der = prev_der + (2 * order - 1) * curr_val
        prev_val, curr_val = (curr_val, next_val)
        prev_der, curr_der = (curr_der, next_der)
    return (curr_val, curr_der)


def second_derivative(value):
    leg_val, leg_der = legendre_pair(value)
    return (2.0 * value * leg_der - 56.0 * leg_val) / (1.0 - value * value)


def basis_tables():
    guesses = [
        -0.8717401485096066,
        -0.5917001814331423,
        -0.2092992179024789,
        0.2092992179024789,
        0.5917001814331423,
        0.8717401485096066,
    ]
    inner_pts = []
    for guess in guesses:
        point = guess
        for newton in range(4):
            point = point - legendre_pair(point)[1] / second_derivative(point)
        inner_pts.append(point)
    gll_points = [-1.0] + inner_pts + [1.0]
    leg_values = [legendre_pair(point)[0] for point in gll_points]
    weights = [2.0 / (56.0 * lv * lv) for lv in leg_values]
    derivative = [[0.0] * 8 for row_at in range(8)]
    for row_at in range(8):
        for col_at in range(8):
            if row_at != col_at:
                derivative[row_at][col_at] = leg_values[row_at] / (
                    leg_values[col_at] * (gll_points[row_at] - gll_points[col_at])
                )
    derivative[0][0] = -14.0
    derivative[7][7] = 14.0
    stiffness = [
        [
            sum(
                (
                    derivative[mid][row_at] * weights[mid] * derivative[mid][col_at]
                    for mid in range(8)
                )
            )
            for col_at in range(8)
        ]
        for row_at in range(8)
    ]
    inv_sqrt = [1.0 / math.sqrt(wt) for wt in weights]
    matrix = [
        [inv_sqrt[row_at] * stiffness[row_at][col_at] * inv_sqrt[col_at] for col_at in range(8)]
        for row_at in range(8)
    ]
    vectors = [[1.0 if row_at == col_at else 0.0 for col_at in range(8)] for row_at in range(8)]
    for sweep in range(14):
        for first in range(8):
            for second in range(first + 1, 8):
                angle = 0.5 * math.atan2(
                    2.0 * matrix[first][second], matrix[second][second] - matrix[first][first]
                )
                cosine = math.cos(angle)
                sine = math.sin(angle)
                for other in range(8):
                    left_val = matrix[other][first]
                    right_val = matrix[other][second]
                    matrix[other][first] = cosine * left_val - sine * right_val
                    matrix[other][second] = sine * left_val + cosine * right_val
                for other in range(8):
                    left_val = matrix[first][other]
                    right_val = matrix[second][other]
                    matrix[first][other] = cosine * left_val - sine * right_val
                    matrix[second][other] = sine * left_val + cosine * right_val
                for other in range(8):
                    left_val = vectors[other][first]
                    right_val = vectors[other][second]
                    vectors[other][first] = cosine * left_val - sine * right_val
                    vectors[other][second] = sine * left_val + cosine * right_val
    eigen_vals = [max(matrix[idx_at][idx_at], 0.0) for idx_at in range(8)]
    eigen_modes = [
        [inv_sqrt[row_at] * vectors[row_at][col_at] for col_at in range(8)] for row_at in range(8)
    ]
    return (weights, stiffness, eigen_modes, eigen_vals)


WEIGHTS, STIFF, MODES, LAMS = basis_tables()
EVEN = [MODES[0][m] * MODES[7][m] > 0 for m in range(8)]


def split_table(table):
    high = table.astype(ml_dtypes.bfloat16)
    low = (table - high.astype(np.float64)).astype(ml_dtypes.bfloat16)
    return [high, low]


def plane_tables():
    modes, stiff, weights = np.array(MODES), np.array(STIFF), np.diag(WEIGHTS)
    four = np.eye(4)
    forward = np.kron(four, np.kron(modes.T, modes.T))
    backward = np.kron(four, np.kron(modes, modes))
    along_j = np.kron(four, np.kron(stiff, weights))
    along_k = np.kron(four, np.kron(weights, stiff))
    solve = np.stack(split_table(forward) + split_table(backward))
    local = np.stack(split_table(along_j) + split_table(along_k))
    return solve, local


def rows(i, j):
    return slice((i * 8 + j) * 8, (i * 8 + j) * 8 + 8)


def plane(n):
    return slice(n * 64, n * 64 + 64)


def eight(n):
    return slice(n * 8, n * 8 + 8)


def lanes(x):
    return slice(x * 128, x * 128 + 128)


def weighted(values, factors):
    total = None
    for value, factor in zip(values, factors):
        term = value * factor
        total = term if total is None else total + term
    return total


def halves(v):
    return [v[a] + v[7 - a] for a in range(4)], [v[a] - v[7 - a] for a in range(4)]


def to_modes(v):
    even, odd = halves(v)
    return [weighted(even if EVEN[m] else odd, [MODES[a][m] for a in range(4)]) for m in range(8)]


def from_modes(t):
    out = [None] * 8
    for a in range(4):
        even = weighted([t[m] for m in range(8) if EVEN[m]], [MODES[a][m] for m in range(8) if EVEN[m]])
        odd = weighted([t[m] for m in range(8) if not EVEN[m]], [MODES[a][m] for m in range(8) if not EVEN[m]])
        out[a], out[7 - a] = even + odd, even - odd
    return out


def stiff_line(v):
    even, odd = halves(v)
    out = [None] * 8
    for i in range(4):
        first = weighted(even, [0.5 * (STIFF[i][a] + STIFF[i][7 - a]) for a in range(4)])
        second = weighted(odd, [0.5 * (STIFF[i][a] - STIFF[i][7 - a]) for a in range(4)])
        out[i], out[7 - i] = first + second, first - second
    return out


def store_split(high_ref, low_ref, row, column, parts):
    chunk = jnp.concatenate(parts, axis=0)
    high = chunk.astype(BF16)
    low = (chunk - high.astype(F32)).astype(BF16)
    high_ref[row : row + 16, column] = high
    low_ref[row : row + 16, column] = low


def product(table, at, high, low):
    dot = functools.partial(jnp.dot, preferred_element_type=F32)
    return dot(table[at], high) + dot(table[at], low) + dot(table[at + 1], high)


def z_summed(ref):
    lane = lax.broadcasted_iota(jnp.int32, (8, 128), 1)
    for x in range(2):
        for i in range(8):
            first = ref[x, pl.ds(i * 64, 8, stride=8), :]
            last = ref[x, pl.ds(i * 64 + 7, 8, stride=8), :]
            ref[x, pl.ds(i * 64, 8, stride=8), :] = jnp.where(lane == 0, 0.0, first + pltpu.roll(last, 1, 1))
            ref[x, pl.ds(i * 64 + 7, 8, stride=8), :] = jnp.where(lane == 127, 0.0, last + pltpu.roll(first, 127, 1))


def x_joined(ref):
    both = ref[0, plane(7), :] + ref[1, plane(0), :]
    ref[0, plane(7), :] = both
    ref[1, plane(0), :] = both


def y_faces(ref, low_ref, high_ref):
    for x in range(2):
        for i in range(8):
            low_ref[x, eight(i), :] = ref[x, rows(i, 0), :]
            high_ref[x, eight(i), :] = ref[x, rows(i, 7), :]


def y_joined(value, x, i, j, before, after, coef):
    if j == 0:
        value = (value + before[x, eight(i), :]) * coef[0, 4]
    if j == 7:
        value = (value + after[x, eight(i), :]) * coef[1, 4]
    return value


def sublane_table(values):
    at = lax.broadcasted_iota(jnp.int32, (8, 128), 0)
    out = jnp.full((8, 128), values[7], F32)
    for n in range(7):
        out = jnp.where(at == n, values[n], out)
    return out


def over_sublanes(row):
    return jnp.broadcast_to(row, (8, 128))


def reversed_points(src, mid, out, orient):
    for x in range(2):
        code = over_sublanes(orient[x : x + 1, :])
        flip_i, flip_j, flip_k = (code & 1) != 0, (code & 2) != 0, (code & 4) != 0
        for i in range(4):
            for j in range(4):
                a, b = src[x, rows(i, j), :], src[x, rows(7 - i, j), :]
                c, d = src[x, rows(i, 7 - j), :], src[x, rows(7 - i, 7 - j), :]
                a, b = jnp.where(flip_i, b, a), jnp.where(flip_i, a, b)
                c, d = jnp.where(flip_i, d, c), jnp.where(flip_i, c, d)
                mid[x, rows(i, j), :] = jnp.where(flip_j, c, a)
                mid[x, rows(i, 7 - j), :] = jnp.where(flip_j, a, c)
                mid[x, rows(7 - i, j), :] = jnp.where(flip_j, d, b)
                mid[x, rows(7 - i, 7 - j), :] = jnp.where(flip_j, b, d)
        for i in range(8):
            for k in range(4):
                a = mid[x, pl.ds(i * 64 + k, 8, stride=8), :]
                b = mid[x, pl.ds(i * 64 + 7 - k, 8, stride=8), :]
                out[x, pl.ds(i * 64 + k, 8, stride=8), :] = jnp.where(flip_k, b, a)
                out[x, pl.ds(i * 64 + 7 - k, 8, stride=8), :] = jnp.where(flip_k, a, b)


def start_kernel(ends, size_x_in, size_y_in, load_in, orient_in, size_z_in, *refs):
    field, y_low, y_high, x_low, x_high, coef, orient, mid, load, length_ref, x_ref, y_ref, ready = refs
    copies = [
        pltpu.make_async_copy(load_in, load, ready.at[0]),
        pltpu.make_async_copy(orient_in, orient, ready.at[1]),
        pltpu.make_async_copy(size_z_in, length_ref, ready.at[2]),
        pltpu.make_async_copy(size_x_in, x_ref, ready.at[3]),
        pltpu.make_async_copy(size_y_in, y_ref, ready.at[4]),
    ]
    for copy in copies:
        copy.start()
    for copy in copies[1:]:
        copy.wait()
    node, dev = lax.axis_index("node"), lax.axis_index("dev")
    inside = [jnp.where(at_end, 0.0, 1.0).astype(F32) for at_end in (node == 0, node == ends[0], dev == 0, dev == ends[1])]
    size_y = y_ref[0]
    length = over_sublanes(length_ref[...])
    weight_k = sublane_table(WEIGHTS)
    lam_k = sublane_table(LAMS)
    at = lax.broadcasted_iota(jnp.int32, (8, 128), 0)
    for x in range(2):
        size_x = x_ref[x]
        coef_x = size_y * length / (2.0 * jnp.full((8, 128), size_x, F32))
        coef_y = size_x * length / (2.0 * jnp.full((8, 128), size_y, F32))
        coef_z = jnp.full((8, 128), size_x * size_y, F32) / (2.0 * length)
        coef[x, 0] = jnp.where(at == 0, coef_x, jnp.where(at == 1, coef_y, coef_z))
        coef[x, 1] = coef_x * weight_k
        coef[x, 2] = lam_k * coef_z + (coef_x + coef_y + coef_z) / 3.0
        coef[x, 3] = jnp.full((8, 128), inside[x], F32)
        coef[x, 4] = jnp.full((8, 128), inside[2 + x], F32)
        coef[x, 5] = weight_k
    copies[0].wait()
    reversed_points(load, mid, field, orient)
    z_summed(field)
    x_joined(field)
    y_faces(field, y_low, y_high)
    x_low[0:64, :] = field[0, plane(0), :]
    x_high[0:64, :] = field[1, plane(7), :]
    x_low[64:72, :] = coef[0, 0]
    x_high[64:72, :] = coef[1, 0]


def edge_kernel(x_low, x_high, before, after, low_out, high_out):
    low_out[...] = x_low[...]
    high_out[...] = x_high[...]
    low_out[0:8, :] += before[0, 0:8, :]
    low_out[56:64, :] += after[0, 0:8, :]
    high_out[0:8, :] += before[1, 56:64, :]
    high_out[56:64, :] += after[1, 56:64, :]


def solve_kernel(with_x, *refs):
    coef, table, field, before, after = refs[:5]
    refs = refs[5:]
    if with_x:
        x_before, x_after = refs[:2]
        refs = refs[2:]
    joined, out, y_low, y_high, dot, high, low, mid = refs
    for x in range(2):
        for pair in range(4):
            lines = []
            for j in (2 * pair, 2 * pair + 1):
                line = []
                for i in range(8):
                    value = y_joined(field[x, rows(i, j), :], x, i, j, before, after, coef)
                    if with_x and x == 0 and i == 0:
                        value = (value + x_before[eight(j), :]) * coef[0, 3] * (
                            coef[0, 4] if j == 0 else coef[1, 4] if j == 7 else 1.0
                        )
                    if with_x and x == 1 and i == 7:
                        value = (value + x_after[eight(j), :]) * coef[1, 3] * (
                            coef[0, 4] if j == 0 else coef[1, 4] if j == 7 else 1.0
                        )
                    joined[x, rows(i, j), :] = value
                    line.append(value)
                lines.append(to_modes(line))
            for m in range(8):
                store_split(high, low, m * 64 + pair * 16, lanes(x), [lines[0][m], lines[1][m]])
    for block in range(2):
        part = slice(block * 256, block * 256 + 256)
        mid[part, :] = product(table, 0, high[part, :], low[part, :])
    for x in range(2):
        coef_x, coef_y = over_sublanes(coef[x, 0, 0:1, :]), over_sublanes(coef[x, 0, 1:2, :])
        den_i = [coef_x * LAMS[m] for m in range(8)]
        den_j = [coef_y * LAMS[n] + coef[x, 2] for n in range(8)]
        for m in range(8):
            for pair in range(4):
                parts = [mid[rows(m, n), lanes(x)] / (den_i[m] + den_j[n]) for n in (2 * pair, 2 * pair + 1)]
                store_split(high, low, m * 64 + pair * 16, lanes(x), parts)
    for block in range(2):
        part = slice(block * 256, block * 256 + 256)
        mid[part, :] = product(table, 2, high[part, :], low[part, :])
    total = jnp.zeros((8, 128), F32)
    for x in range(2):
        for j in range(8):
            line = from_modes([mid[rows(m, j), lanes(x)] for m in range(8)])
            for i in range(8):
                out[x, rows(i, j), :] = line[i]
                total = total + line[i] * joined[x, rows(i, j), :]
    dot[...] = total
    z_summed(out)
    x_joined(out)
    y_faces(out, y_low, y_high)


def local_kernel(coef, table, field, before, after, joined, out, x_low, x_high, high, low, first, second):
    for x in range(2):
        for pair in range(4):
            for i in range(8):
                parts = []
                for j in (2 * pair, 2 * pair + 1):
                    value = y_joined(field[x, rows(i, j), :], x, i, j, before, after, coef)
                    if x == 0 and i == 0:
                        value = value * coef[0, 3]
                    if x == 1 and i == 7:
                        value = value * coef[1, 3]
                    joined[x, rows(i, j), :] = value
                    parts.append(value)
                store_split(high, low, i * 64 + pair * 16, lanes(x), parts)
    for block in range(2):
        part = slice(block * 256, block * 256 + 256)
        first[part, :] = product(table, 0, high[part, :], low[part, :])
        second[part, :] = product(table, 2, high[part, :], low[part, :])
    for x in range(2):
        coef_y, coef_z = over_sublanes(coef[x, 0, 1:2, :]), over_sublanes(coef[x, 0, 2:3, :])
        for j in range(8):
            scale = coef[x, 1] * WEIGHTS[j]
            line = stiff_line([joined[x, rows(i, j), :] for i in range(8)])
            for i in range(8):
                flat = coef_y * first[rows(i, j), lanes(x)] + coef_z * second[rows(i, j), lanes(x)]
                out[x, rows(i, j), :] = scale * line[i] + WEIGHTS[i] * flat
    x_low[0:64, :] = joined[0, plane(0), :]
    x_low[64:128, :] = out[0, plane(0), :]
    x_high[0:64, :] = joined[1, plane(7), :]
    x_high[64:128, :] = out[1, plane(7), :]


def cross_kernel(with_row, *refs):
    coef, table, field, local, x_before, x_after, kind_before, kind_after = refs[:8]
    refs = refs[8:]
    if with_row:
        earlier = refs[:3]
        refs = refs[3:]
    joined, out, y_low, y_high, dot, high, low, first, second = refs
    joined[...] = field[...]
    for pair in range(4):
        parts = [[], [], [], []]
        for j in (2 * pair, 2 * pair + 1):
            for side in range(2):
                own = field[side, rows(7 * side, j), :]
                came = (x_after if side else x_before)[eight(j), :] * coef[side, 3]
                joined[side, rows(7 * side, j), :] = own + came
                parts[side].append(came)
                parts[2 + side].append(own)
        for n in range(4):
            store_split(high, low, n * 64 + pair * 16, slice(0, 128), parts[n])
    first[...] = product(table, 0, high[...], low[...])
    second[...] = product(table, 2, high[...], low[...])
    total = jnp.zeros((8, 128), F32)
    for side in range(2):
        end = 7 * side
        coef_y, coef_z = over_sublanes(coef[side, 0, 1:2, :]), over_sublanes(coef[side, 0, 2:3, :])
        kind, sent = (kind_after, x_after) if side else (kind_before, x_before)
        far_x, far_y, far_z = [over_sublanes(kind[64 + n : 65 + n, :]) for n in range(3)]
        for j in range(8):
            came = sent[eight(j), :] * coef[side, 3]
            own = field[side, rows(end, j), :]
            pulled = coef[side, 1] * WEIGHTS[j] * came
            for i in range(8):
                value = local[side, rows(i, j), :] + STIFF[i][end] * pulled
                if i == end:
                    flat = coef_y * first[rows(side, j), :] + coef_z * second[rows(side, j), :]
                    value = value + WEIGHTS[end] * flat
                total = total + value * joined[side, rows(i, j), :]
                if i == end:
                    far = sent[64 + j * 8 : 72 + j * 8, :]
                    far = far + (STIFF[7 - end][7 - end] * WEIGHTS[j]) * (far_x * coef[side, 5]) * own
                    flat = far_y * first[rows(2 + side, j), :] + far_z * second[rows(2 + side, j), :]
                    far = far + WEIGHTS[7 - end] * flat
                    value = (value + far) * coef[side, 3]
                out[side, rows(i, j), :] = value
    z_summed(out)
    x_joined(out)
    y_faces(out, y_low, y_high)
    if with_row:
        lane = lax.broadcasted_iota(jnp.int32, (8, 128), 1)
        row = jnp.zeros((8, 128), F32)
        for n, value in enumerate([ref[...] for ref in earlier] + [total]):
            value = value + pltpu.roll(value, 64, 1)
            value = value + pltpu.roll(value, 32, 1)
            row = jnp.where(lane // 32 == n, value, row)
        row = over_sublanes(jnp.sum(row, axis=0, keepdims=True))
        for n in range(dot.shape[0] // 8):
            dot[eight(n), :] = row
    else:
        dot[...] = total


def sum_kernel(parts, out):
    row = over_sublanes(jnp.sum(parts[...], axis=0, keepdims=True))
    for n in range(out.shape[0] // 8):
        out[eight(n), :] = row


def end_kernel(coef, orient, sums, last, before, after, load, first, image, second, answer, rest, one, two):
    lane = lax.broadcasted_iota(jnp.int32, (8, 128), 1)
    row = jnp.sum(sums[...], axis=0, keepdims=True)
    dots = [jnp.full((8, 128), jnp.sum(jnp.where(lane[0:1, :] // 32 == n, row, 0.0)), F32) for n in range(4)]
    alpha = dots[0] / dots[1]
    energy = dots[0] - 2.0 * alpha * dots[1] + alpha * alpha * dots[2]
    keep = 1.0 + energy / dots[0]
    curve = keep * keep * dots[1] - 2.0 * alpha * keep * dots[2] + alpha * alpha * dots[3]
    step = energy / curve
    on_first = alpha + step * keep
    on_second = step * alpha
    for x in range(2):
        for i in range(8):
            for j in range(8):
                at = rows(i, j)
                value = y_joined(last[x, at, :], x, i, j, before, after, coef)
                one[x, at, :] = on_first * first[x, at, :] - on_second * second[x, at, :]
                two[x, at, :] = load[x, at, :] - on_first * image[x, at, :] + on_second * value
    reversed_points(one, one, answer, orient)
    reversed_points(two, two, rest, orient)


def f32(*shape):
    return jax.ShapeDtypeStruct(shape, F32)


def call(kernel, outs, scratch, *args, spaces=(), room=24):
    return pl.pallas_call(
        kernel,
        out_shape=outs,
        in_specs=[pl.BlockSpec(memory_space=space) for space in spaces]
        + [pl.BlockSpec(memory_space=pltpu.VMEM)] * (len(args) - len(spaces)),
        out_specs=jax.tree.map(lambda _: pl.BlockSpec(memory_space=pltpu.VMEM), outs),
        scratch_shapes=scratch,
        compiler_params=pltpu.CompilerParams(vmem_limit_bytes=room * 1024 * 1024),
    )(*args)


FIELD = f32(2, 512, 128)
FACES = [f32(2, 64, 128)] * 2
EIGHT = f32(8, 128)


def kept_in_hbm(x):
    return pltpu.with_memory_space_constraint(x, pltpu.HBM)


def swap_y(low, high):
    return passed_along(high, "dev", 1), passed_along(low, "dev", -1)


def swap_x(low, high):
    return passed_along(high, "node", 1), passed_along(low, "node", -1)


def exchanged(rows_out, axis):
    came = lax.all_to_all(rows_out.reshape(-1, 1, 128), axis, 0, 0)
    return came.reshape(rows_out.shape)


def shards(element_load, orient, size_x, size_y, size_z):
    solve_np, local_np = plane_tables()
    solve_table, local_table = jnp.asarray(solve_np), jnp.asarray(local_np)
    nodes, devs = lax.axis_size("node"), lax.axis_size("dev")
    field, y_low, y_high, x_low, x_high, coef, orient = call(
        functools.partial(start_kernel, (nodes - 1, devs - 1)),
        [FIELD, *FACES, f32(72, 128), f32(72, 128), f32(2, 8, 8, 128), jax.ShapeDtypeStruct((2, 128), jnp.int32)],
        [
            pltpu.VMEM((2, 512, 128), F32),
            pltpu.VMEM((2, 512, 128), F32),
            pltpu.VMEM((1, 128), F32),
            pltpu.SMEM((2,), F32),
            pltpu.SMEM((1,), F32),
            pltpu.SemaphoreType.DMA((5,)),
        ],
        size_x, size_y,
        *map(kept_in_hbm, (element_load.reshape(2, 512, 128), orient.reshape(2, 128), size_z.reshape(1, 128))),
        spaces=[pltpu.HBM] * 5,
    )
    y_came = swap_y(y_low, y_high)
    x_faces = call(edge_kernel, [f32(72, 128)] * 2, [], x_low, x_high, *y_came)
    kinds = swap_x(*x_faces)

    def solved(field, y_came, x_came):
        joined, out, low, high, dot = call(
            functools.partial(solve_kernel, bool(x_came)),
            [FIELD, FIELD, *FACES, EIGHT],
            [pltpu.VMEM((512, 256), BF16)] * 2 + [pltpu.VMEM((512, 256), F32)],
            coef, solve_table, field, *y_came, *x_came,
        )
        return joined, out, swap_y(low, high), dot

    def applied(field, y_came, earlier):
        joined, local, low, high = call(
            local_kernel,
            [FIELD, FIELD, f32(128, 128), f32(128, 128)],
            [pltpu.VMEM((512, 256), BF16)] * 2 + [pltpu.VMEM((512, 256), F32)] * 2,
            coef, local_table, field, *y_came,
        )
        x_came = swap_x(low, high)
        joined, out, low, high, dot = call(
            functools.partial(cross_kernel, bool(earlier)),
            [FIELD, FIELD, *FACES, f32(64, 128) if earlier else EIGHT],
            [pltpu.VMEM((256, 128), BF16)] * 2 + [pltpu.VMEM((256, 128), F32)] * 2,
            coef, local_table, joined, local, *x_came, *kinds, *earlier,
        )
        return joined, out, (low, high), dot

    load, out, y_came, dot_a = solved(field, y_came, kinds)
    first, out, faces, dot_c = applied(out, y_came, ())
    image, out, y_came, dot_d = solved(out, swap_y(*faces), ())
    second, out, (low, high), row = applied(out, y_came, (dot_a, dot_c, dot_d))
    before, after = swap_y(low, high)
    row = call(sum_kernel, f32(8, 128), [], exchanged(row, "dev"))
    row = exchanged(row, "node")
    answer, rest = call(
        end_kernel,
        [FIELD, FIELD],
        [pltpu.VMEM((2, 512, 128), F32)] * 2,
        coef, orient, row, out, before, after, load, first, image, second,
    )
    return answer.reshape(element_load.shape), rest.reshape(element_load.shape)


def solution(mesh):
    return jax.shard_map(
        shards,
        mesh=mesh,
        in_specs=(
            P("node", "dev", None, None, None, None),
            P("node", "dev", None),
            P("node"),
            P("dev"),
            P(),
        ),
        out_specs=(
            P("node", "dev", None, None, None, None),
            P("node", "dev", None, None, None, None),
        ),
        check_vma=False,
    )
```

```python
import functools
import math

import jax
import jax.numpy as jnp
import ml_dtypes
import numpy as np
from jax import lax
from jax.experimental import pallas as pl
from jax.experimental.pallas import tpu as pltpu
from jax.sharding import PartitionSpec as P

F32 = jnp.float32
BF16 = jnp.bfloat16


def passed_along(x, axis, by):
    peers = lax.axis_size(axis)
    return lax.ppermute(x, axis, [(i, (i + by) % peers) for i in range(peers)])


def legendre_pair(value):
    prev_val = 1.0
    curr_val = value
    prev_der = 0.0
    curr_der = 1.0
    for order in range(2, 8):
        next_val = ((2 * order - 1) * value * curr_val - (order - 1) * prev_val) / order
        next_der = prev_der + (2 * order - 1) * curr_val
        prev_val, curr_val = (curr_val, next_val)
        prev_der, curr_der = (curr_der, next_der)
    return (curr_val, curr_der)


def second_derivative(value):
    leg_val, leg_der = legendre_pair(value)
    return (2.0 * value * leg_der - 56.0 * leg_val) / (1.0 - value * value)


def basis_tables():
    guesses = [
        -0.8717401485096066,
        -0.5917001814331423,
        -0.2092992179024789,
        0.2092992179024789,
        0.5917001814331423,
        0.8717401485096066,
    ]
    inner_pts = []
    for guess in guesses:
        point = guess
        for newton in range(4):
            point = point - legendre_pair(point)[1] / second_derivative(point)
        inner_pts.append(point)
    gll_points = [-1.0] + inner_pts + [1.0]
    leg_values = [legendre_pair(point)[0] for point in gll_points]
    weights = [2.0 / (56.0 * lv * lv) for lv in leg_values]
    derivative = [[0.0] * 8 for row_at in range(8)]
    for row_at in range(8):
        for col_at in range(8):
            if row_at != col_at:
                derivative[row_at][col_at] = leg_values[row_at] / (
                    leg_values[col_at] * (gll_points[row_at] - gll_points[col_at])
                )
    derivative[0][0] = -14.0
    derivative[7][7] = 14.0
    stiffness = [
        [
            sum(
                (
                    derivative[mid][row_at] * weights[mid] * derivative[mid][col_at]
                    for mid in range(8)
                )
            )
            for col_at in range(8)
        ]
        for row_at in range(8)
    ]
    inv_sqrt = [1.0 / math.sqrt(wt) for wt in weights]
    matrix = [
        [inv_sqrt[row_at] * stiffness[row_at][col_at] * inv_sqrt[col_at] for col_at in range(8)]
        for row_at in range(8)
    ]
    vectors = [[1.0 if row_at == col_at else 0.0 for col_at in range(8)] for row_at in range(8)]
    for sweep in range(14):
        for first in range(8):
            for second in range(first + 1, 8):
                angle = 0.5 * math.atan2(
                    2.0 * matrix[first][second], matrix[second][second] - matrix[first][first]
                )
                cosine = math.cos(angle)
                sine = math.sin(angle)
                for other in range(8):
                    left_val = matrix[other][first]
                    right_val = matrix[other][second]
                    matrix[other][first] = cosine * left_val - sine * right_val
                    matrix[other][second] = sine * left_val + cosine * right_val
                for other in range(8):
                    left_val = matrix[first][other]
                    right_val = matrix[second][other]
                    matrix[first][other] = cosine * left_val - sine * right_val
                    matrix[second][other] = sine * left_val + cosine * right_val
                for other in range(8):
                    left_val = vectors[other][first]
                    right_val = vectors[other][second]
                    vectors[other][first] = cosine * left_val - sine * right_val
                    vectors[other][second] = sine * left_val + cosine * right_val
    eigen_vals = [max(matrix[idx_at][idx_at], 0.0) for idx_at in range(8)]
    eigen_modes = [
        [inv_sqrt[row_at] * vectors[row_at][col_at] for col_at in range(8)] for row_at in range(8)
    ]
    return (weights, stiffness, eigen_modes, eigen_vals)


WEIGHTS, STIFF, MODES, LAMS = basis_tables()
EVEN = [MODES[0][m] * MODES[7][m] > 0 for m in range(8)]


def split_table(table):
    high = table.astype(ml_dtypes.bfloat16)
    low = (table - high.astype(np.float64)).astype(ml_dtypes.bfloat16)
    return [high, low]


def plane_tables():
    modes, stiff, weights = np.array(MODES), np.array(STIFF), np.diag(WEIGHTS)
    four = np.eye(4)
    forward = np.kron(four, np.kron(modes.T, modes.T))
    backward = np.kron(four, np.kron(modes, modes))
    along_j = np.kron(four, np.kron(stiff, weights))
    along_k = np.kron(four, np.kron(weights, stiff))
    solve = np.stack(split_table(forward) + split_table(backward))
    local = np.stack(split_table(along_j) + split_table(along_k))
    return solve, local


def rows(i, j):
    return slice((i * 8 + j) * 8, (i * 8 + j) * 8 + 8)


def plane(n):
    return slice(n * 64, n * 64 + 64)


def eight(n):
    return slice(n * 8, n * 8 + 8)


def lanes(x):
    return slice(x * 128, x * 128 + 128)


def weighted(values, factors):
    total = None
    for value, factor in zip(values, factors):
        term = value * factor
        total = term if total is None else total + term
    return total


def halves(v):
    return [v[a] + v[7 - a] for a in range(4)], [v[a] - v[7 - a] for a in range(4)]


def to_modes(v):
    even, odd = halves(v)
    return [weighted(even if EVEN[m] else odd, [MODES[a][m] for a in range(4)]) for m in range(8)]


def from_modes(t):
    out = [None] * 8
    for a in range(4):
        even = weighted([t[m] for m in range(8) if EVEN[m]], [MODES[a][m] for m in range(8) if EVEN[m]])
        odd = weighted([t[m] for m in range(8) if not EVEN[m]], [MODES[a][m] for m in range(8) if not EVEN[m]])
        out[a], out[7 - a] = even + odd, even - odd
    return out


def stiff_line(v):
    even, odd = halves(v)
    out = [None] * 8
    for i in range(4):
        first = weighted(even, [0.5 * (STIFF[i][a] + STIFF[i][7 - a]) for a in range(4)])
        second = weighted(odd, [0.5 * (STIFF[i][a] - STIFF[i][7 - a]) for a in range(4)])
        out[i], out[7 - i] = first + second, first - second
    return out


def store_split(high_ref, low_ref, row, column, parts):
    chunk = jnp.concatenate(parts, axis=0)
    high = chunk.astype(BF16)
    low = (chunk - high.astype(F32)).astype(BF16)
    high_ref[row : row + 16, column] = high
    low_ref[row : row + 16, column] = low


def product(table, at, high, low):
    dot = functools.partial(jnp.dot, preferred_element_type=F32)
    return dot(table[at], high) + dot(table[at], low) + dot(table[at + 1], high)


def z_summed(ref):
    lane = lax.broadcasted_iota(jnp.int32, (8, 128), 1)
    for x in range(2):
        for i in range(8):
            first = ref[x, pl.ds(i * 64, 8, stride=8), :]
            last = ref[x, pl.ds(i * 64 + 7, 8, stride=8), :]
            ref[x, pl.ds(i * 64, 8, stride=8), :] = jnp.where(lane == 0, 0.0, first + pltpu.roll(last, 1, 1))
            ref[x, pl.ds(i * 64 + 7, 8, stride=8), :] = jnp.where(lane == 127, 0.0, last + pltpu.roll(first, 127, 1))


def x_joined(ref):
    both = ref[0, plane(7), :] + ref[1, plane(0), :]
    ref[0, plane(7), :] = both
    ref[1, plane(0), :] = both


def is_odd(coef):
    return coef[0, 6] > 0.5


def y_faces(ref, pair_ref, other_ref, coef):
    odd = is_odd(coef)
    for x in range(2):
        for i in range(8):
            low, high = ref[x, rows(i, 0), :], ref[x, rows(i, 7), :]
            pair_ref[x, eight(i), :] = jnp.where(odd, low, high)
            other_ref[x, eight(i), :] = jnp.where(odd, high, low)


def face_came(x, i, end, pair, other, coef):
    odd = is_odd(coef)
    first, second = (other, pair) if end == 0 else (pair, other)
    return jnp.where(odd, second[x, eight(i), :], first[x, eight(i), :])


def y_joined(value, x, i, j, other, pair, coef):
    if j == 0:
        value = (value + face_came(x, i, 0, pair, other, coef)) * coef[0, 4]
    if j == 7:
        value = (value + face_came(x, i, 7, pair, other, coef)) * coef[1, 4]
    return value


def sublane_table(values):
    at = lax.broadcasted_iota(jnp.int32, (8, 128), 0)
    out = jnp.full((8, 128), values[7], F32)
    for n in range(7):
        out = jnp.where(at == n, values[n], out)
    return out


def over_sublanes(row):
    return jnp.broadcast_to(row, (8, 128))


def reversed_points(src, mid, out, orient):
    for x in range(2):
        code = over_sublanes(orient[x : x + 1, :])
        flip_i, flip_j, flip_k = (code & 1) != 0, (code & 2) != 0, (code & 4) != 0
        for i in range(4):
            for j in range(4):
                a, b = src[x, rows(i, j), :], src[x, rows(7 - i, j), :]
                c, d = src[x, rows(i, 7 - j), :], src[x, rows(7 - i, 7 - j), :]
                a, b = jnp.where(flip_i, b, a), jnp.where(flip_i, a, b)
                c, d = jnp.where(flip_i, d, c), jnp.where(flip_i, c, d)
                mid[x, rows(i, j), :] = jnp.where(flip_j, c, a)
                mid[x, rows(i, 7 - j), :] = jnp.where(flip_j, a, c)
                mid[x, rows(7 - i, j), :] = jnp.where(flip_j, d, b)
                mid[x, rows(7 - i, 7 - j), :] = jnp.where(flip_j, b, d)
        for i in range(8):
            for k in range(4):
                a = mid[x, pl.ds(i * 64 + k, 8, stride=8), :]
                b = mid[x, pl.ds(i * 64 + 7 - k, 8, stride=8), :]
                out[x, pl.ds(i * 64 + k, 8, stride=8), :] = jnp.where(flip_k, b, a)
                out[x, pl.ds(i * 64 + 7 - k, 8, stride=8), :] = jnp.where(flip_k, a, b)


def start_kernel(ends, size_x_in, size_y_in, load_in, orient_in, size_z_in, *refs):
    field, y_low, y_high, x_low, x_high, coef, orient, mid, load, length_ref, x_ref, y_ref, ready = refs
    copies = [
        pltpu.make_async_copy(load_in, load, ready.at[0]),
        pltpu.make_async_copy(orient_in, orient, ready.at[1]),
        pltpu.make_async_copy(size_z_in, length_ref, ready.at[2]),
        pltpu.make_async_copy(size_x_in, x_ref, ready.at[3]),
        pltpu.make_async_copy(size_y_in, y_ref, ready.at[4]),
    ]
    for copy in copies:
        copy.start()
    for copy in copies[1:]:
        copy.wait()
    node, dev = lax.axis_index("node"), lax.axis_index("dev")
    inside = [jnp.where(at_end, 0.0, 1.0).astype(F32) for at_end in (node == 0, node == ends[0], dev == 0, dev == ends[1])]
    size_y = y_ref[0]
    length = over_sublanes(length_ref[...])
    weight_k = sublane_table(WEIGHTS)
    lam_k = sublane_table(LAMS)
    at = lax.broadcasted_iota(jnp.int32, (8, 128), 0)
    for x in range(2):
        size_x = x_ref[x]
        coef_x = size_y * length / (2.0 * jnp.full((8, 128), size_x, F32))
        coef_y = size_x * length / (2.0 * jnp.full((8, 128), size_y, F32))
        coef_z = jnp.full((8, 128), size_x * size_y, F32) / (2.0 * length)
        coef[x, 0] = jnp.where(at == 0, coef_x, jnp.where(at == 1, coef_y, coef_z))
        coef[x, 1] = coef_x * weight_k
        coef[x, 2] = lam_k * coef_z + (coef_x + coef_y + coef_z) / 3.0
        coef[x, 3] = jnp.full((8, 128), inside[x], F32)
        coef[x, 4] = jnp.full((8, 128), inside[2 + x], F32)
        coef[x, 5] = weight_k
        coef[x, 6] = jnp.full((8, 128), jnp.where(dev % 2 == 1, 1.0, 0.0), F32)
    copies[0].wait()
    reversed_points(load, mid, field, orient)
    z_summed(field)
    x_joined(field)
    y_faces(field, y_low, y_high, coef)
    x_low[0:64, :] = field[0, plane(0), :]
    x_high[0:64, :] = field[1, plane(7), :]
    x_low[64:72, :] = coef[0, 0]
    x_high[64:72, :] = coef[1, 0]


def edge_kernel(coef, x_low, x_high, other, pair, low_out, high_out):
    low_out[...] = x_low[...]
    high_out[...] = x_high[...]
    low_out[0:8, :] += face_came(0, 0, 0, pair, other, coef)
    low_out[56:64, :] += face_came(0, 0, 7, pair, other, coef)
    high_out[0:8, :] += face_came(1, 7, 0, pair, other, coef)
    high_out[56:64, :] += face_came(1, 7, 7, pair, other, coef)


def solve_kernel(with_x, *refs):
    coef, table, field, before, after = refs[:5]
    refs = refs[5:]
    if with_x:
        x_before, x_after = refs[:2]
        refs = refs[2:]
    joined, out, y_low, y_high, dot, high, low, mid = refs
    for x in range(2):
        for pair in range(4):
            lines = []
            for j in (2 * pair, 2 * pair + 1):
                line = []
                for i in range(8):
                    value = y_joined(field[x, rows(i, j), :], x, i, j, before, after, coef)
                    if with_x and x == 0 and i == 0:
                        value = (value + x_before[eight(j), :]) * coef[0, 3] * (
                            coef[0, 4] if j == 0 else coef[1, 4] if j == 7 else 1.0
                        )
                    if with_x and x == 1 and i == 7:
                        value = (value + x_after[eight(j), :]) * coef[1, 3] * (
                            coef[0, 4] if j == 0 else coef[1, 4] if j == 7 else 1.0
                        )
                    joined[x, rows(i, j), :] = value
                    line.append(value)
                lines.append(to_modes(line))
            for m in range(8):
                store_split(high, low, m * 64 + pair * 16, lanes(x), [lines[0][m], lines[1][m]])
    for block in range(2):
        part = slice(block * 256, block * 256 + 256)
        mid[part, :] = product(table, 0, high[part, :], low[part, :])
    for x in range(2):
        coef_x, coef_y = over_sublanes(coef[x, 0, 0:1, :]), over_sublanes(coef[x, 0, 1:2, :])
        den_i = [coef_x * LAMS[m] for m in range(8)]
        den_j = [coef_y * LAMS[n] + coef[x, 2] for n in range(8)]
        for m in range(8):
            for pair in range(4):
                parts = [mid[rows(m, n), lanes(x)] / (den_i[m] + den_j[n]) for n in (2 * pair, 2 * pair + 1)]
                store_split(high, low, m * 64 + pair * 16, lanes(x), parts)
    for block in range(2):
        part = slice(block * 256, block * 256 + 256)
        mid[part, :] = product(table, 2, high[part, :], low[part, :])
    total = jnp.zeros((8, 128), F32)
    for x in range(2):
        for j in range(8):
            line = from_modes([mid[rows(m, j), lanes(x)] for m in range(8)])
            for i in range(8):
                out[x, rows(i, j), :] = line[i]
                total = total + line[i] * joined[x, rows(i, j), :]
    dot[...] = total
    z_summed(out)
    x_joined(out)
    y_faces(out, y_low, y_high, coef)


def local_kernel(coef, table, field, before, after, joined, out, x_low, x_high, high, low, first, second):
    for x in range(2):
        for pair in range(4):
            for i in range(8):
                parts = []
                for j in (2 * pair, 2 * pair + 1):
                    value = y_joined(field[x, rows(i, j), :], x, i, j, before, after, coef)
                    if x == 0 and i == 0:
                        value = value * coef[0, 3]
                    if x == 1 and i == 7:
                        value = value * coef[1, 3]
                    joined[x, rows(i, j), :] = value
                    parts.append(value)
                store_split(high, low, i * 64 + pair * 16, lanes(x), parts)
    for block in range(2):
        part = slice(block * 256, block * 256 + 256)
        first[part, :] = product(table, 0, high[part, :], low[part, :])
        second[part, :] = product(table, 2, high[part, :], low[part, :])
    for x in range(2):
        coef_y, coef_z = over_sublanes(coef[x, 0, 1:2, :]), over_sublanes(coef[x, 0, 2:3, :])
        for j in range(8):
            scale = coef[x, 1] * WEIGHTS[j]
            line = stiff_line([joined[x, rows(i, j), :] for i in range(8)])
            for i in range(8):
                flat = coef_y * first[rows(i, j), lanes(x)] + coef_z * second[rows(i, j), lanes(x)]
                out[x, rows(i, j), :] = scale * line[i] + WEIGHTS[i] * flat
    x_low[0:64, :] = joined[0, plane(0), :]
    x_low[64:128, :] = out[0, plane(0), :]
    x_high[0:64, :] = joined[1, plane(7), :]
    x_high[64:128, :] = out[1, plane(7), :]


def cross_kernel(with_row, *refs):
    coef, table, field, local, x_before, x_after, kind_before, kind_after = refs[:8]
    refs = refs[8:]
    if with_row:
        earlier = refs[:3]
        refs = refs[3:]
    joined, out, y_low, y_high, dot, high, low, first, second = refs
    joined[...] = field[...]
    for pair in range(4):
        parts = [[], [], [], []]
        for j in (2 * pair, 2 * pair + 1):
            for side in range(2):
                own = field[side, rows(7 * side, j), :]
                came = (x_after if side else x_before)[eight(j), :] * coef[side, 3]
                joined[side, rows(7 * side, j), :] = own + came
                parts[side].append(came)
                parts[2 + side].append(own)
        for n in range(4):
            store_split(high, low, n * 64 + pair * 16, slice(0, 128), parts[n])
    first[...] = product(table, 0, high[...], low[...])
    second[...] = product(table, 2, high[...], low[...])
    total = jnp.zeros((8, 128), F32)
    for side in range(2):
        end = 7 * side
        coef_y, coef_z = over_sublanes(coef[side, 0, 1:2, :]), over_sublanes(coef[side, 0, 2:3, :])
        kind, sent = (kind_after, x_after) if side else (kind_before, x_before)
        far_x, far_y, far_z = [over_sublanes(kind[64 + n : 65 + n, :]) for n in range(3)]
        for j in range(8):
            came = sent[eight(j), :] * coef[side, 3]
            own = field[side, rows(end, j), :]
            pulled = coef[side, 1] * WEIGHTS[j] * came
            for i in range(8):
                value = local[side, rows(i, j), :] + STIFF[i][end] * pulled
                if i == end:
                    flat = coef_y * first[rows(side, j), :] + coef_z * second[rows(side, j), :]
                    value = value + WEIGHTS[end] * flat
                total = total + value * joined[side, rows(i, j), :]
                if i == end:
                    far = sent[64 + j * 8 : 72 + j * 8, :]
                    far = far + (STIFF[7 - end][7 - end] * WEIGHTS[j]) * (far_x * coef[side, 5]) * own
                    flat = far_y * first[rows(2 + side, j), :] + far_z * second[rows(2 + side, j), :]
                    far = far + WEIGHTS[7 - end] * flat
                    value = (value + far) * coef[side, 3]
                out[side, rows(i, j), :] = value
    z_summed(out)
    x_joined(out)
    y_faces(out, y_low, y_high, coef)
    if with_row:
        lane = lax.broadcasted_iota(jnp.int32, (8, 128), 1)
        row = jnp.zeros((8, 128), F32)
        for n, value in enumerate([ref[...] for ref in earlier] + [total]):
            value = value + pltpu.roll(value, 64, 1)
            value = value + pltpu.roll(value, 32, 1)
            row = jnp.where(lane // 32 == n, value, row)
        row = over_sublanes(jnp.sum(row, axis=0, keepdims=True))
        for n in range(dot.shape[0] // 8):
            dot[eight(n), :] = row
    else:
        dot[...] = total


def sum_kernel(parts, out):
    row = over_sublanes(jnp.sum(parts[...], axis=0, keepdims=True))
    for n in range(out.shape[0] // 8):
        out[eight(n), :] = row


def end_kernel(coef, orient, sums, last, before, after, load, first, image, second, answer, rest, one, two):
    lane = lax.broadcasted_iota(jnp.int32, (8, 128), 1)
    row = jnp.sum(sums[...], axis=0, keepdims=True)
    dots = [jnp.full((8, 128), jnp.sum(jnp.where(lane[0:1, :] // 32 == n, row, 0.0)), F32) for n in range(4)]
    alpha = dots[0] / dots[1]
    energy = dots[0] - 2.0 * alpha * dots[1] + alpha * alpha * dots[2]
    keep = 1.0 + energy / dots[0]
    curve = keep * keep * dots[1] - 2.0 * alpha * keep * dots[2] + alpha * alpha * dots[3]
    step = energy / curve
    on_first = alpha + step * keep
    on_second = step * alpha
    for x in range(2):
        for i in range(8):
            for j in range(8):
                at = rows(i, j)
                value = y_joined(last[x, at, :], x, i, j, before, after, coef)
                one[x, at, :] = on_first * first[x, at, :] - on_second * second[x, at, :]
                two[x, at, :] = load[x, at, :] - on_first * image[x, at, :] + on_second * value
    reversed_points(one, one, answer, orient)
    reversed_points(two, two, rest, orient)


def f32(*shape):
    return jax.ShapeDtypeStruct(shape, F32)


def call(kernel, outs, scratch, *args, spaces=(), room=24):
    return pl.pallas_call(
        kernel,
        out_shape=outs,
        in_specs=[pl.BlockSpec(memory_space=space) for space in spaces]
        + [pl.BlockSpec(memory_space=pltpu.VMEM)] * (len(args) - len(spaces)),
        out_specs=jax.tree.map(lambda _: pl.BlockSpec(memory_space=pltpu.VMEM), outs),
        scratch_shapes=scratch,
        compiler_params=pltpu.CompilerParams(vmem_limit_bytes=room * 1024 * 1024),
    )(*args)


FIELD = f32(2, 512, 128)
FACES = [f32(2, 64, 128)] * 2
EIGHT = f32(8, 128)


def kept_in_hbm(x):
    return pltpu.with_memory_space_constraint(x, pltpu.HBM)


def swap_y(pair, other):
    devs = lax.axis_size("dev")
    far = lax.ppermute(other, "dev", [(i, i - 1 if i % 2 == 0 else i + 1) for i in range(1, devs - 1)])
    near = lax.ppermute(pair, "dev", [(i, i + 1 if i % 2 == 0 else i - 1) for i in range(devs)])
    return far, near


def swap_x(low, high):
    return passed_along(high, "node", 1), passed_along(low, "node", -1)


def exchanged(rows_out, axis):
    came = lax.all_to_all(rows_out.reshape(-1, 1, 128), axis, 0, 0)
    return came.reshape(rows_out.shape)


def shards(element_load, orient, size_x, size_y, size_z):
    solve_np, local_np = plane_tables()
    solve_table, local_table = jnp.asarray(solve_np), jnp.asarray(local_np)
    nodes, devs = lax.axis_size("node"), lax.axis_size("dev")
    field, y_low, y_high, x_low, x_high, coef, orient = call(
        functools.partial(start_kernel, (nodes - 1, devs - 1)),
        [FIELD, *FACES, f32(72, 128), f32(72, 128), f32(2, 8, 8, 128), jax.ShapeDtypeStruct((2, 128), jnp.int32)],
        [
            pltpu.VMEM((2, 512, 128), F32),
            pltpu.VMEM((2, 512, 128), F32),
            pltpu.VMEM((1, 128), F32),
            pltpu.SMEM((2,), F32),
            pltpu.SMEM((1,), F32),
            pltpu.SemaphoreType.DMA((5,)),
        ],
        kept_in_hbm(size_x), size_y,
        *map(kept_in_hbm, (element_load.reshape(2, 512, 128), orient.reshape(2, 128), size_z.reshape(1, 128))),
        spaces=[pltpu.HBM] * 5,
    )
    y_came = swap_y(y_low, y_high)
    x_faces = call(edge_kernel, [f32(72, 128)] * 2, [], coef, x_low, x_high, *y_came)
    kinds = swap_x(*x_faces)

    def solved(field, y_came, x_came):
        joined, out, low, high, dot = call(
            functools.partial(solve_kernel, bool(x_came)),
            [FIELD, FIELD, *FACES, EIGHT],
            [pltpu.VMEM((512, 256), BF16)] * 2 + [pltpu.VMEM((512, 256), F32)],
            coef, solve_table, field, *y_came, *x_came,
        )
        return joined, out, swap_y(low, high), dot

    def applied(field, y_came, earlier):
        joined, local, low, high = call(
            local_kernel,
            [FIELD, FIELD, f32(128, 128), f32(128, 128)],
            [pltpu.VMEM((512, 256), BF16)] * 2 + [pltpu.VMEM((512, 256), F32)] * 2,
            coef, local_table, field, *y_came,
        )
        x_came = swap_x(low, high)
        joined, out, low, high, dot = call(
            functools.partial(cross_kernel, bool(earlier)),
            [FIELD, FIELD, *FACES, pltpu.VMEM((64, 128), F32) if earlier else EIGHT],
            [pltpu.VMEM((256, 128), BF16)] * 2 + [pltpu.VMEM((256, 128), F32)] * 2,
            coef, local_table, joined, local, *x_came, *kinds, *earlier,
        )
        return joined, out, (low, high), dot

    load, out, y_came, dot_a = solved(field, y_came, kinds)
    first, out, faces, dot_c = applied(out, y_came, ())
    image, out, y_came, dot_d = solved(out, swap_y(*faces), ())
    second, out, (low, high), row = applied(out, y_came, (dot_a, dot_c, dot_d))
    before, after = swap_y(low, high)
    row = call(sum_kernel, pltpu.VMEM((8, 128), F32), [], exchanged(row, "dev"))
    row = exchanged(row, "node")
    answer, rest = call(
        end_kernel,
        [FIELD, FIELD],
        [pltpu.VMEM((2, 512, 128), F32)] * 2,
        coef, orient, row, out, before, after, load, first, image, second,
    )
    return answer.reshape(element_load.shape), rest.reshape(element_load.shape)


def solution(mesh):
    return jax.shard_map(
        shards,
        mesh=mesh,
        in_specs=(
            P("node", "dev", None, None, None, None),
            P("node", "dev", None),
            P("node"),
            P("dev"),
            P(),
        ),
        out_specs=(
            P("node", "dev", None, None, None, None),
            P("node", "dev", None, None, None, None),
        ),
        check_vma=False,
    )
```

```python
import functools
import math

import jax
import jax.numpy as jnp
import ml_dtypes
import numpy as np
from jax import lax
from jax.experimental import pallas as pl
from jax.experimental.pallas import tpu as pltpu
from jax.sharding import PartitionSpec as P

F32 = jnp.float32
BF16 = jnp.bfloat16


def passed_along(x, axis, by):
    peers = lax.axis_size(axis)
    return lax.ppermute(x, axis, [(i, (i + by) % peers) for i in range(peers)])


def legendre_pair(value):
    prev_val = 1.0
    curr_val = value
    prev_der = 0.0
    curr_der = 1.0
    for order in range(2, 8):
        next_val = ((2 * order - 1) * value * curr_val - (order - 1) * prev_val) / order
        next_der = prev_der + (2 * order - 1) * curr_val
        prev_val, curr_val = (curr_val, next_val)
        prev_der, curr_der = (curr_der, next_der)
    return (curr_val, curr_der)


def second_derivative(value):
    leg_val, leg_der = legendre_pair(value)
    return (2.0 * value * leg_der - 56.0 * leg_val) / (1.0 - value * value)


def basis_tables():
    guesses = [
        -0.8717401485096066,
        -0.5917001814331423,
        -0.2092992179024789,
        0.2092992179024789,
        0.5917001814331423,
        0.8717401485096066,
    ]
    inner_pts = []
    for guess in guesses:
        point = guess
        for newton in range(4):
            point = point - legendre_pair(point)[1] / second_derivative(point)
        inner_pts.append(point)
    gll_points = [-1.0] + inner_pts + [1.0]
    leg_values = [legendre_pair(point)[0] for point in gll_points]
    weights = [2.0 / (56.0 * lv * lv) for lv in leg_values]
    derivative = [[0.0] * 8 for row_at in range(8)]
    for row_at in range(8):
        for col_at in range(8):
            if row_at != col_at:
                derivative[row_at][col_at] = leg_values[row_at] / (
                    leg_values[col_at] * (gll_points[row_at] - gll_points[col_at])
                )
    derivative[0][0] = -14.0
    derivative[7][7] = 14.0
    stiffness = [
        [
            sum(
                (
                    derivative[mid][row_at] * weights[mid] * derivative[mid][col_at]
                    for mid in range(8)
                )
            )
            for col_at in range(8)
        ]
        for row_at in range(8)
    ]
    inv_sqrt = [1.0 / math.sqrt(wt) for wt in weights]
    matrix = [
        [inv_sqrt[row_at] * stiffness[row_at][col_at] * inv_sqrt[col_at] for col_at in range(8)]
        for row_at in range(8)
    ]
    vectors = [[1.0 if row_at == col_at else 0.0 for col_at in range(8)] for row_at in range(8)]
    for sweep in range(14):
        for first in range(8):
            for second in range(first + 1, 8):
                angle = 0.5 * math.atan2(
                    2.0 * matrix[first][second], matrix[second][second] - matrix[first][first]
                )
                cosine = math.cos(angle)
                sine = math.sin(angle)
                for other in range(8):
                    left_val = matrix[other][first]
                    right_val = matrix[other][second]
                    matrix[other][first] = cosine * left_val - sine * right_val
                    matrix[other][second] = sine * left_val + cosine * right_val
                for other in range(8):
                    left_val = matrix[first][other]
                    right_val = matrix[second][other]
                    matrix[first][other] = cosine * left_val - sine * right_val
                    matrix[second][other] = sine * left_val + cosine * right_val
                for other in range(8):
                    left_val = vectors[other][first]
                    right_val = vectors[other][second]
                    vectors[other][first] = cosine * left_val - sine * right_val
                    vectors[other][second] = sine * left_val + cosine * right_val
    eigen_vals = [max(matrix[idx_at][idx_at], 0.0) for idx_at in range(8)]
    eigen_modes = [
        [inv_sqrt[row_at] * vectors[row_at][col_at] for col_at in range(8)] for row_at in range(8)
    ]
    return (weights, stiffness, eigen_modes, eigen_vals)


WEIGHTS, STIFF, MODES, LAMS = basis_tables()
EVEN = [MODES[0][m] * MODES[7][m] > 0 for m in range(8)]


def split_table(table):
    high = table.astype(ml_dtypes.bfloat16)
    low = (table - high.astype(np.float64)).astype(ml_dtypes.bfloat16)
    return [high, low]


def plane_tables():
    modes, stiff, weights = np.array(MODES), np.array(STIFF), np.diag(WEIGHTS)
    four = np.eye(4)
    forward = np.kron(four, np.kron(modes.T, modes.T))
    backward = np.kron(four, np.kron(modes, modes))
    along_j = np.kron(four, np.kron(stiff, weights))
    along_k = np.kron(four, np.kron(weights, stiff))
    solve = np.stack(split_table(forward) + split_table(backward))
    local = np.stack(split_table(along_j) + split_table(along_k))
    return solve, local


def rows(i, j):
    return slice((i * 8 + j) * 8, (i * 8 + j) * 8 + 8)


def plane(n):
    return slice(n * 64, n * 64 + 64)


def eight(n):
    return slice(n * 8, n * 8 + 8)


def lanes(x):
    return slice(x * 128, x * 128 + 128)


def weighted(values, factors):
    total = None
    for value, factor in zip(values, factors):
        term = value * factor
        total = term if total is None else total + term
    return total


def halves(v):
    return [v[a] + v[7 - a] for a in range(4)], [v[a] - v[7 - a] for a in range(4)]


def to_modes(v):
    even, odd = halves(v)
    return [weighted(even if EVEN[m] else odd, [MODES[a][m] for a in range(4)]) for m in range(8)]


def from_modes(t):
    out = [None] * 8
    for a in range(4):
        even = weighted([t[m] for m in range(8) if EVEN[m]], [MODES[a][m] for m in range(8) if EVEN[m]])
        odd = weighted([t[m] for m in range(8) if not EVEN[m]], [MODES[a][m] for m in range(8) if not EVEN[m]])
        out[a], out[7 - a] = even + odd, even - odd
    return out


def stiff_line(v):
    even, odd = halves(v)
    out = [None] * 8
    for i in range(4):
        first = weighted(even, [0.5 * (STIFF[i][a] + STIFF[i][7 - a]) for a in range(4)])
        second = weighted(odd, [0.5 * (STIFF[i][a] - STIFF[i][7 - a]) for a in range(4)])
        out[i], out[7 - i] = first + second, first - second
    return out


def store_split(high_ref, low_ref, row, column, parts):
    chunk = jnp.concatenate(parts, axis=0)
    high = chunk.astype(BF16)
    low = (chunk - high.astype(F32)).astype(BF16)
    high_ref[row : row + 16, column] = high
    low_ref[row : row + 16, column] = low


def product(table, at, high, low):
    dot = functools.partial(jnp.dot, preferred_element_type=F32)
    return dot(table[at], high) + dot(table[at], low) + dot(table[at + 1], high)


def z_summed(ref):
    lane = lax.broadcasted_iota(jnp.int32, (8, 128), 1)
    for x in range(2):
        for i in range(8):
            first = ref[x, pl.ds(i * 64, 8, stride=8), :]
            last = ref[x, pl.ds(i * 64 + 7, 8, stride=8), :]
            ref[x, pl.ds(i * 64, 8, stride=8), :] = jnp.where(lane == 0, 0.0, first + pltpu.roll(last, 1, 1))
            ref[x, pl.ds(i * 64 + 7, 8, stride=8), :] = jnp.where(lane == 127, 0.0, last + pltpu.roll(first, 127, 1))


def x_joined(ref):
    both = ref[0, plane(7), :] + ref[1, plane(0), :]
    ref[0, plane(7), :] = both
    ref[1, plane(0), :] = both


def is_odd(coef):
    return coef[0, 6] > 0.5


def y_faces(ref, pair_ref, other_ref, coef):
    odd = is_odd(coef)
    for x in range(2):
        for i in range(8):
            low, high = ref[x, rows(i, 0), :], ref[x, rows(i, 7), :]
            pair_ref[x, eight(i), :] = jnp.where(odd, low, high)
            other_ref[x, eight(i), :] = jnp.where(odd, high, low)


def face_came(x, i, end, pair, other, coef):
    odd = is_odd(coef)
    first, second = (other, pair) if end == 0 else (pair, other)
    return jnp.where(odd, second[x, eight(i), :], first[x, eight(i), :])


def y_joined(value, x, i, j, other, pair, coef):
    if j == 0:
        value = (value + face_came(x, i, 0, pair, other, coef)) * coef[0, 4]
    if j == 7:
        value = (value + face_came(x, i, 7, pair, other, coef)) * coef[1, 4]
    return value


def sublane_table(values):
    at = lax.broadcasted_iota(jnp.int32, (8, 128), 0)
    out = jnp.full((8, 128), values[7], F32)
    for n in range(7):
        out = jnp.where(at == n, values[n], out)
    return out


def over_sublanes(row):
    return jnp.broadcast_to(row, (8, 128))


def reversed_points(src, mid, out, orient, columns=(0, 1)):
    for x in columns:
        code = over_sublanes(orient[x : x + 1, :])
        flip_i, flip_j, flip_k = (code & 1) != 0, (code & 2) != 0, (code & 4) != 0
        for i in range(4):
            for j in range(4):
                a, b = src[x, rows(i, j), :], src[x, rows(7 - i, j), :]
                c, d = src[x, rows(i, 7 - j), :], src[x, rows(7 - i, 7 - j), :]
                a, b = jnp.where(flip_i, b, a), jnp.where(flip_i, a, b)
                c, d = jnp.where(flip_i, d, c), jnp.where(flip_i, c, d)
                mid[x, rows(i, j), :] = jnp.where(flip_j, c, a)
                mid[x, rows(i, 7 - j), :] = jnp.where(flip_j, a, c)
                mid[x, rows(7 - i, j), :] = jnp.where(flip_j, d, b)
                mid[x, rows(7 - i, 7 - j), :] = jnp.where(flip_j, b, d)
        for i in range(8):
            for k in range(4):
                a = mid[x, pl.ds(i * 64 + k, 8, stride=8), :]
                b = mid[x, pl.ds(i * 64 + 7 - k, 8, stride=8), :]
                out[x, pl.ds(i * 64 + k, 8, stride=8), :] = jnp.where(flip_k, b, a)
                out[x, pl.ds(i * 64 + 7 - k, 8, stride=8), :] = jnp.where(flip_k, a, b)


def start_kernel(ends, size_x_in, size_y_in, load_in, orient_in, size_z_in, *refs):
    field, y_low, y_high, x_low, x_high, coef, orient, mid, load, length_ref, x_ref, y_ref, ready = refs
    copies = [
        pltpu.make_async_copy(load_in.at[0], load.at[0], ready.at[0]),
        pltpu.make_async_copy(orient_in, orient, ready.at[1]),
        pltpu.make_async_copy(size_z_in, length_ref, ready.at[2]),
        pltpu.make_async_copy(size_x_in, x_ref, ready.at[3]),
        pltpu.make_async_copy(size_y_in, y_ref, ready.at[4]),
        pltpu.make_async_copy(load_in.at[1], load.at[1], ready.at[5]),
    ]
    for copy in copies:
        copy.start()
    for copy in copies[1:5]:
        copy.wait()
    node, dev = lax.axis_index("node"), lax.axis_index("dev")
    inside = [jnp.where(at_end, 0.0, 1.0).astype(F32) for at_end in (node == 0, node == ends[0], dev == 0, dev == ends[1])]
    size_y = y_ref[0]
    length = over_sublanes(length_ref[...])
    weight_k = sublane_table(WEIGHTS)
    lam_k = sublane_table(LAMS)
    at = lax.broadcasted_iota(jnp.int32, (8, 128), 0)
    for x in range(2):
        size_x = x_ref[x]
        coef_x = size_y * length / (2.0 * jnp.full((8, 128), size_x, F32))
        coef_y = size_x * length / (2.0 * jnp.full((8, 128), size_y, F32))
        coef_z = jnp.full((8, 128), size_x * size_y, F32) / (2.0 * length)
        coef[x, 0] = jnp.where(at == 0, coef_x, jnp.where(at == 1, coef_y, coef_z))
        coef[x, 1] = coef_x * weight_k
        coef[x, 2] = lam_k * coef_z + (coef_x + coef_y + coef_z) / 3.0
        coef[x, 3] = jnp.full((8, 128), inside[x], F32)
        coef[x, 4] = jnp.full((8, 128), inside[2 + x], F32)
        coef[x, 5] = weight_k
        coef[x, 6] = jnp.full((8, 128), jnp.where(dev % 2 == 1, 1.0, 0.0), F32)
    copies[0].wait()
    reversed_points(load, mid, field, orient, (0,))
    copies[5].wait()
    reversed_points(load, mid, field, orient, (1,))
    z_summed(field)
    x_joined(field)
    y_faces(field, y_low, y_high, coef)
    x_low[0:64, :] = field[0, plane(0), :]
    x_high[0:64, :] = field[1, plane(7), :]
    x_low[64:72, :] = coef[0, 0]
    x_high[64:72, :] = coef[1, 0]


def edge_kernel(coef, x_low, x_high, other, pair, low_out, high_out):
    low_out[...] = x_low[...]
    high_out[...] = x_high[...]
    low_out[0:8, :] += face_came(0, 0, 0, pair, other, coef)
    low_out[56:64, :] += face_came(0, 0, 7, pair, other, coef)
    high_out[0:8, :] += face_came(1, 7, 0, pair, other, coef)
    high_out[56:64, :] += face_came(1, 7, 7, pair, other, coef)


def solve_kernel(with_x, *refs):
    coef, table, field, before, after = refs[:5]
    refs = refs[5:]
    if with_x:
        x_before, x_after = refs[:2]
        refs = refs[2:]
    joined, out, y_low, y_high, dot, high, low, mid = refs
    for x in range(2):
        for pair in range(4):
            lines = []
            for j in (2 * pair, 2 * pair + 1):
                line = []
                for i in range(8):
                    value = y_joined(field[x, rows(i, j), :], x, i, j, before, after, coef)
                    if with_x and x == 0 and i == 0:
                        value = (value + x_before[eight(j), :]) * coef[0, 3] * (
                            coef[0, 4] if j == 0 else coef[1, 4] if j == 7 else 1.0
                        )
                    if with_x and x == 1 and i == 7:
                        value = (value + x_after[eight(j), :]) * coef[1, 3] * (
                            coef[0, 4] if j == 0 else coef[1, 4] if j == 7 else 1.0
                        )
                    joined[x, rows(i, j), :] = value
                    line.append(value)
                lines.append(to_modes(line))
            for m in range(8):
                store_split(high, low, m * 64 + pair * 16, lanes(x), [lines[0][m], lines[1][m]])
    for block in range(2):
        part = slice(block * 256, block * 256 + 256)
        mid[part, :] = product(table, 0, high[part, :], low[part, :])
    for x in range(2):
        coef_x, coef_y = over_sublanes(coef[x, 0, 0:1, :]), over_sublanes(coef[x, 0, 1:2, :])
        den_i = [coef_x * LAMS[m] for m in range(8)]
        den_j = [coef_y * LAMS[n] + coef[x, 2] for n in range(8)]
        for m in range(8):
            for pair in range(4):
                parts = [mid[rows(m, n), lanes(x)] / (den_i[m] + den_j[n]) for n in (2 * pair, 2 * pair + 1)]
                store_split(high, low, m * 64 + pair * 16, lanes(x), parts)
    for block in range(2):
        part = slice(block * 256, block * 256 + 256)
        mid[part, :] = product(table, 2, high[part, :], low[part, :])
    total = jnp.zeros((8, 128), F32)
    for x in range(2):
        for j in range(8):
            line = from_modes([mid[rows(m, j), lanes(x)] for m in range(8)])
            for i in range(8):
                out[x, rows(i, j), :] = line[i]
                total = total + line[i] * joined[x, rows(i, j), :]
    dot[...] = total
    z_summed(out)
    x_joined(out)
    y_faces(out, y_low, y_high, coef)


def local_kernel(coef, table, field, before, after, joined, out, x_low, x_high, high, low, first, second):
    for x in range(2):
        for pair in range(4):
            for i in range(8):
                parts = []
                for j in (2 * pair, 2 * pair + 1):
                    value = y_joined(field[x, rows(i, j), :], x, i, j, before, after, coef)
                    if x == 0 and i == 0:
                        value = value * coef[0, 3]
                    if x == 1 and i == 7:
                        value = value * coef[1, 3]
                    joined[x, rows(i, j), :] = value
                    parts.append(value)
                store_split(high, low, i * 64 + pair * 16, lanes(x), parts)
    for block in range(2):
        part = slice(block * 256, block * 256 + 256)
        first[part, :] = product(table, 0, high[part, :], low[part, :])
        second[part, :] = product(table, 2, high[part, :], low[part, :])
    for x in range(2):
        coef_y, coef_z = over_sublanes(coef[x, 0, 1:2, :]), over_sublanes(coef[x, 0, 2:3, :])
        for j in range(8):
            scale = coef[x, 1] * WEIGHTS[j]
            line = stiff_line([joined[x, rows(i, j), :] for i in range(8)])
            for i in range(8):
                flat = coef_y * first[rows(i, j), lanes(x)] + coef_z * second[rows(i, j), lanes(x)]
                out[x, rows(i, j), :] = scale * line[i] + WEIGHTS[i] * flat
    x_low[0:64, :] = joined[0, plane(0), :]
    x_low[64:128, :] = out[0, plane(0), :]
    x_high[0:64, :] = joined[1, plane(7), :]
    x_high[64:128, :] = out[1, plane(7), :]


def cross_kernel(with_row, *refs):
    coef, table, field, local, x_before, x_after, kind_before, kind_after = refs[:8]
    refs = refs[8:]
    if with_row:
        earlier = refs[:3]
        refs = refs[3:]
    joined, out, y_low, y_high, dot, high, low, first, second = refs
    joined[...] = field[...]
    for pair in range(4):
        parts = [[], [], [], []]
        for j in (2 * pair, 2 * pair + 1):
            for side in range(2):
                own = field[side, rows(7 * side, j), :]
                came = (x_after if side else x_before)[eight(j), :] * coef[side, 3]
                joined[side, rows(7 * side, j), :] = own + came
                parts[side].append(came)
                parts[2 + side].append(own)
        for n in range(4):
            store_split(high, low, n * 64 + pair * 16, slice(0, 128), parts[n])
    first[...] = product(table, 0, high[...], low[...])
    second[...] = product(table, 2, high[...], low[...])
    total = jnp.zeros((8, 128), F32)
    for side in range(2):
        end = 7 * side
        coef_y, coef_z = over_sublanes(coef[side, 0, 1:2, :]), over_sublanes(coef[side, 0, 2:3, :])
        kind, sent = (kind_after, x_after) if side else (kind_before, x_before)
        far_x, far_y, far_z = [over_sublanes(kind[64 + n : 65 + n, :]) for n in range(3)]
        for j in range(8):
            came = sent[eight(j), :] * coef[side, 3]
            own = field[side, rows(end, j), :]
            pulled = coef[side, 1] * WEIGHTS[j] * came
            for i in range(8):
                value = local[side, rows(i, j), :] + STIFF[i][end] * pulled
                if i == end:
                    flat = coef_y * first[rows(side, j), :] + coef_z * second[rows(side, j), :]
                    value = value + WEIGHTS[end] * flat
                total = total + value * joined[side, rows(i, j), :]
                if i == end:
                    far = sent[64 + j * 8 : 72 + j * 8, :]
                    far = far + (STIFF[7 - end][7 - end] * WEIGHTS[j]) * (far_x * coef[side, 5]) * own
                    flat = far_y * first[rows(2 + side, j), :] + far_z * second[rows(2 + side, j), :]
                    far = far + WEIGHTS[7 - end] * flat
                    value = (value + far) * coef[side, 3]
                out[side, rows(i, j), :] = value
    z_summed(out)
    x_joined(out)
    y_faces(out, y_low, y_high, coef)
    if with_row:
        lane = lax.broadcasted_iota(jnp.int32, (8, 128), 1)
        row = jnp.zeros((8, 128), F32)
        for n, value in enumerate([ref[...] for ref in earlier] + [total]):
            value = value + pltpu.roll(value, 64, 1)
            value = value + pltpu.roll(value, 32, 1)
            row = jnp.where(lane // 32 == n, value, row)
        row = over_sublanes(jnp.sum(row, axis=0, keepdims=True))
        for n in range(dot.shape[0] // 8):
            dot[eight(n), :] = row
    else:
        dot[...] = total


def sum_kernel(parts, out):
    row = over_sublanes(jnp.sum(parts[...], axis=0, keepdims=True))
    for n in range(out.shape[0] // 8):
        out[eight(n), :] = row


def end_kernel(coef, orient, sums, last, before, after, load, first, image, second, answer, rest, one, two, sent):
    lane = lax.broadcasted_iota(jnp.int32, (8, 128), 1)
    row = jnp.sum(sums[...], axis=0, keepdims=True)
    dots = [jnp.full((8, 128), jnp.sum(jnp.where(lane[0:1, :] // 32 == n, row, 0.0)), F32) for n in range(4)]
    alpha = dots[0] / dots[1]
    energy = dots[0] - 2.0 * alpha * dots[1] + alpha * alpha * dots[2]
    keep = 1.0 + energy / dots[0]
    curve = keep * keep * dots[1] - 2.0 * alpha * keep * dots[2] + alpha * alpha * dots[3]
    step = energy / curve
    on_first = alpha + step * keep
    on_second = step * alpha
    copies = []
    for x in range(2):
        for i in range(8):
            for j in range(8):
                at = rows(i, j)
                one[x, at, :] = on_first * first[x, at, :] - on_second * second[x, at, :]
        reversed_points(one, one, one, orient, (x,))
        copies.append(pltpu.make_async_copy(one.at[x], answer.at[x], sent.at[x, 0]))
        copies[-1].start()
        for i in range(8):
            for j in range(8):
                at = rows(i, j)
                value = y_joined(last[x, at, :], x, i, j, before, after, coef)
                two[x, at, :] = load[x, at, :] - on_first * image[x, at, :] + on_second * value
        reversed_points(two, two, two, orient, (x,))
        copies.append(pltpu.make_async_copy(two.at[x], rest.at[x], sent.at[x, 1]))
        copies[-1].start()
    for copy in copies:
        copy.wait()


def f32(*shape):
    return jax.ShapeDtypeStruct(shape, F32)


def call(kernel, outs, scratch, *args, spaces=(), room=24, out_space=pltpu.VMEM):
    return pl.pallas_call(
        kernel,
        out_shape=outs,
        in_specs=[pl.BlockSpec(memory_space=space) for space in spaces]
        + [pl.BlockSpec(memory_space=pltpu.VMEM)] * (len(args) - len(spaces)),
        out_specs=jax.tree.map(lambda _: pl.BlockSpec(memory_space=out_space), outs),
        scratch_shapes=scratch,
        compiler_params=pltpu.CompilerParams(vmem_limit_bytes=room * 1024 * 1024),
    )(*args)


FIELD = f32(2, 512, 128)
FACES = [f32(2, 64, 128)] * 2
EIGHT = f32(8, 128)


def kept_in_hbm(x):
    return pltpu.with_memory_space_constraint(x, pltpu.HBM)


def swap_y(pair, other):
    devs = lax.axis_size("dev")
    far = lax.ppermute(other, "dev", [(i, i - 1 if i % 2 == 0 else i + 1) for i in range(1, devs - 1)])
    near = lax.ppermute(pair, "dev", [(i, i + 1 if i % 2 == 0 else i - 1) for i in range(devs)])
    return far, near


def swap_x(low, high):
    return passed_along(high, "node", 1), passed_along(low, "node", -1)


def exchanged(rows_out, axis):
    came = lax.all_to_all(rows_out.reshape(-1, 1, 128), axis, 0, 0)
    return came.reshape(rows_out.shape)


def shards(element_load, orient, size_x, size_y, size_z):
    solve_np, local_np = plane_tables()
    solve_table, local_table = jnp.asarray(solve_np), jnp.asarray(local_np)
    nodes, devs = lax.axis_size("node"), lax.axis_size("dev")
    field, y_low, y_high, x_low, x_high, coef, orient = call(
        functools.partial(start_kernel, (nodes - 1, devs - 1)),
        [FIELD, *FACES, f32(72, 128), f32(72, 128), f32(2, 8, 8, 128), jax.ShapeDtypeStruct((2, 128), jnp.int32)],
        [
            pltpu.VMEM((2, 512, 128), F32),
            pltpu.VMEM((2, 512, 128), F32),
            pltpu.VMEM((1, 128), F32),
            pltpu.SMEM((2,), F32),
            pltpu.SMEM((1,), F32),
            pltpu.SemaphoreType.DMA((6,)),
        ],
        kept_in_hbm(size_x), size_y,
        *map(kept_in_hbm, (element_load.reshape(2, 512, 128), orient.reshape(2, 128), size_z.reshape(1, 128))),
        spaces=[pltpu.HBM] * 5,
    )
    y_came = swap_y(y_low, y_high)
    x_faces = call(edge_kernel, [f32(72, 128)] * 2, [], coef, x_low, x_high, *y_came)
    kinds = swap_x(*x_faces)

    def solved(field, y_came, x_came):
        joined, out, low, high, dot = call(
            functools.partial(solve_kernel, bool(x_came)),
            [FIELD, FIELD, *FACES, EIGHT],
            [pltpu.VMEM((512, 256), BF16)] * 2 + [pltpu.VMEM((512, 256), F32)],
            coef, solve_table, field, *y_came, *x_came,
        )
        return joined, out, swap_y(low, high), dot

    def applied(field, y_came, earlier):
        joined, local, low, high = call(
            local_kernel,
            [FIELD, FIELD, f32(128, 128), f32(128, 128)],
            [pltpu.VMEM((512, 256), BF16)] * 2 + [pltpu.VMEM((512, 256), F32)] * 2,
            coef, local_table, field, *y_came,
        )
        x_came = swap_x(low, high)
        joined, out, low, high, dot = call(
            functools.partial(cross_kernel, bool(earlier)),
            [FIELD, FIELD, *FACES, pltpu.VMEM((64, 128), F32) if earlier else EIGHT],
            [pltpu.VMEM((256, 128), BF16)] * 2 + [pltpu.VMEM((256, 128), F32)] * 2,
            coef, local_table, joined, local, *x_came, *kinds, *earlier,
        )
        return joined, out, (low, high), dot

    load, out, y_came, dot_a = solved(field, y_came, kinds)
    first, out, faces, dot_c = applied(out, y_came, ())
    image, out, y_came, dot_d = solved(out, swap_y(*faces), ())
    second, out, (low, high), row = applied(out, y_came, (dot_a, dot_c, dot_d))
    before, after = swap_y(low, high)
    row = call(sum_kernel, pltpu.VMEM((8, 128), F32), [], exchanged(row, "dev"))
    row = exchanged(row, "node")
    answer, rest = call(
        end_kernel,
        [FIELD, FIELD],
        [pltpu.VMEM((2, 512, 128), F32)] * 2 + [pltpu.SemaphoreType.DMA((2, 2))],
        coef, orient, row, out, before, after, load, first, image, second,
        out_space=pltpu.HBM,
    )
    return answer.reshape(element_load.shape), rest.reshape(element_load.shape)


def solution(mesh):
    return jax.shard_map(
        shards,
        mesh=mesh,
        in_specs=(
            P("node", "dev", None, None, None, None),
            P("node", "dev", None),
            P("node"),
            P("dev"),
            P(),
        ),
        out_specs=(
            P("node", "dev", None, None, None, None),
            P("node", "dev", None, None, None, None),
        ),
        check_vma=False,
    )
```

```python
import functools
import math

import jax
import jax.numpy as jnp
import ml_dtypes
import numpy as np
from jax import lax
from jax.experimental import pallas as pl
from jax.experimental.pallas import tpu as pltpu
from jax.sharding import PartitionSpec as P

F32 = jnp.float32
BF16 = jnp.bfloat16


def passed_along(x, axis, by):
    peers = lax.axis_size(axis)
    return lax.ppermute(x, axis, [(i, (i + by) % peers) for i in range(peers)])


def legendre_pair(value):
    prev_val = 1.0
    curr_val = value
    prev_der = 0.0
    curr_der = 1.0
    for order in range(2, 8):
        next_val = ((2 * order - 1) * value * curr_val - (order - 1) * prev_val) / order
        next_der = prev_der + (2 * order - 1) * curr_val
        prev_val, curr_val = (curr_val, next_val)
        prev_der, curr_der = (curr_der, next_der)
    return (curr_val, curr_der)


def second_derivative(value):
    leg_val, leg_der = legendre_pair(value)
    return (2.0 * value * leg_der - 56.0 * leg_val) / (1.0 - value * value)


def basis_tables():
    guesses = [
        -0.8717401485096066,
        -0.5917001814331423,
        -0.2092992179024789,
        0.2092992179024789,
        0.5917001814331423,
        0.8717401485096066,
    ]
    inner_pts = []
    for guess in guesses:
        point = guess
        for newton in range(4):
            point = point - legendre_pair(point)[1] / second_derivative(point)
        inner_pts.append(point)
    gll_points = [-1.0] + inner_pts + [1.0]
    leg_values = [legendre_pair(point)[0] for point in gll_points]
    weights = [2.0 / (56.0 * lv * lv) for lv in leg_values]
    derivative = [[0.0] * 8 for row_at in range(8)]
    for row_at in range(8):
        for col_at in range(8):
            if row_at != col_at:
                derivative[row_at][col_at] = leg_values[row_at] / (
                    leg_values[col_at] * (gll_points[row_at] - gll_points[col_at])
                )
    derivative[0][0] = -14.0
    derivative[7][7] = 14.0
    stiffness = [
        [
            sum(
                (
                    derivative[mid][row_at] * weights[mid] * derivative[mid][col_at]
                    for mid in range(8)
                )
            )
            for col_at in range(8)
        ]
        for row_at in range(8)
    ]
    inv_sqrt = [1.0 / math.sqrt(wt) for wt in weights]
    matrix = [
        [inv_sqrt[row_at] * stiffness[row_at][col_at] * inv_sqrt[col_at] for col_at in range(8)]
        for row_at in range(8)
    ]
    vectors = [[1.0 if row_at == col_at else 0.0 for col_at in range(8)] for row_at in range(8)]
    for sweep in range(14):
        for first in range(8):
            for second in range(first + 1, 8):
                angle = 0.5 * math.atan2(
                    2.0 * matrix[first][second], matrix[second][second] - matrix[first][first]
                )
                cosine = math.cos(angle)
                sine = math.sin(angle)
                for other in range(8):
                    left_val = matrix[other][first]
                    right_val = matrix[other][second]
                    matrix[other][first] = cosine * left_val - sine * right_val
                    matrix[other][second] = sine * left_val + cosine * right_val
                for other in range(8):
                    left_val = matrix[first][other]
                    right_val = matrix[second][other]
                    matrix[first][other] = cosine * left_val - sine * right_val
                    matrix[second][other] = sine * left_val + cosine * right_val
                for other in range(8):
                    left_val = vectors[other][first]
                    right_val = vectors[other][second]
                    vectors[other][first] = cosine * left_val - sine * right_val
                    vectors[other][second] = sine * left_val + cosine * right_val
    eigen_vals = [max(matrix[idx_at][idx_at], 0.0) for idx_at in range(8)]
    eigen_modes = [
        [inv_sqrt[row_at] * vectors[row_at][col_at] for col_at in range(8)] for row_at in range(8)
    ]
    return (weights, stiffness, eigen_modes, eigen_vals)


WEIGHTS, STIFF, MODES, LAMS = basis_tables()
EVEN = [MODES[0][m] * MODES[7][m] > 0 for m in range(8)]


def split_table(table):
    high = table.astype(ml_dtypes.bfloat16)
    low = (table - high.astype(np.float64)).astype(ml_dtypes.bfloat16)
    return [high, low]


def plane_tables():
    modes, stiff, weights = np.array(MODES), np.array(STIFF), np.diag(WEIGHTS)
    four = np.eye(4)
    forward = np.kron(four, np.kron(modes.T, modes.T))
    backward = np.kron(four, np.kron(modes, modes))
    along_j = np.kron(four, np.kron(stiff, weights))
    along_k = np.kron(four, np.kron(weights, stiff))
    solve = np.stack(split_table(forward) + split_table(backward))
    local = np.stack(split_table(along_j) + split_table(along_k))
    return solve, local


def rows(i, j):
    return slice((i * 8 + j) * 8, (i * 8 + j) * 8 + 8)


def plane(n):
    return slice(n * 64, n * 64 + 64)


def eight(n):
    return slice(n * 8, n * 8 + 8)


def lanes(x):
    return slice(x * 128, x * 128 + 128)


def weighted(values, factors):
    total = None
    for value, factor in zip(values, factors):
        term = value * factor
        total = term if total is None else total + term
    return total


def halves(v):
    return [v[a] + v[7 - a] for a in range(4)], [v[a] - v[7 - a] for a in range(4)]


def to_modes(v):
    even, odd = halves(v)
    return [weighted(even if EVEN[m] else odd, [MODES[a][m] for a in range(4)]) for m in range(8)]


def from_modes(t):
    out = [None] * 8
    for a in range(4):
        even = weighted([t[m] for m in range(8) if EVEN[m]], [MODES[a][m] for m in range(8) if EVEN[m]])
        odd = weighted([t[m] for m in range(8) if not EVEN[m]], [MODES[a][m] for m in range(8) if not EVEN[m]])
        out[a], out[7 - a] = even + odd, even - odd
    return out


def stiff_line(v):
    even, odd = halves(v)
    out = [None] * 8
    for i in range(4):
        first = weighted(even, [0.5 * (STIFF[i][a] + STIFF[i][7 - a]) for a in range(4)])
        second = weighted(odd, [0.5 * (STIFF[i][a] - STIFF[i][7 - a]) for a in range(4)])
        out[i], out[7 - i] = first + second, first - second
    return out


def store_split(high_ref, low_ref, row, column, parts):
    chunk = jnp.concatenate(parts, axis=0)
    high = chunk.astype(BF16)
    low = (chunk - high.astype(F32)).astype(BF16)
    high_ref[row : row + 16, column] = high
    low_ref[row : row + 16, column] = low


def product(table, at, high, low):
    dot = functools.partial(jnp.dot, preferred_element_type=F32)
    return dot(table[at], high) + dot(table[at], low) + dot(table[at + 1], high)


def z_summed(ref):
    lane = lax.broadcasted_iota(jnp.int32, (8, 128), 1)
    for x in range(2):
        for i in range(8):
            first = ref[x, pl.ds(i * 64, 8, stride=8), :]
            last = ref[x, pl.ds(i * 64 + 7, 8, stride=8), :]
            ref[x, pl.ds(i * 64, 8, stride=8), :] = jnp.where(lane == 0, 0.0, first + pltpu.roll(last, 1, 1))
            ref[x, pl.ds(i * 64 + 7, 8, stride=8), :] = jnp.where(lane == 127, 0.0, last + pltpu.roll(first, 127, 1))


def x_joined(ref):
    both = ref[0, plane(7), :] + ref[1, plane(0), :]
    ref[0, plane(7), :] = both
    ref[1, plane(0), :] = both


def is_odd(coef):
    return coef[0, 6] > 0.5


def y_faces(ref, pair_ref, other_ref, coef):
    odd = is_odd(coef)
    for x in range(2):
        for i in range(8):
            low, high = ref[x, rows(i, 0), :], ref[x, rows(i, 7), :]
            pair_ref[x, eight(i), :] = jnp.where(odd, low, high)
            other_ref[x, eight(i), :] = jnp.where(odd, high, low)


def face_came(x, i, end, pair, other, coef):
    odd = is_odd(coef)
    first, second = (other, pair) if end == 0 else (pair, other)
    return jnp.where(odd, second[x, eight(i), :], first[x, eight(i), :])


def y_joined(value, x, i, j, other, pair, coef):
    if j == 0:
        value = (value + face_came(x, i, 0, pair, other, coef)) * coef[0, 4]
    if j == 7:
        value = (value + face_came(x, i, 7, pair, other, coef)) * coef[1, 4]
    return value


def sublane_table(values):
    at = lax.broadcasted_iota(jnp.int32, (8, 128), 0)
    out = jnp.full((8, 128), values[7], F32)
    for n in range(7):
        out = jnp.where(at == n, values[n], out)
    return out


def over_sublanes(row):
    return jnp.broadcast_to(row, (8, 128))


def reversed_points(src, mid, out, orient, columns=(0, 1)):
    for x in columns:
        code = over_sublanes(orient[x : x + 1, :])
        flip_i, flip_j, flip_k = (code & 1) != 0, (code & 2) != 0, (code & 4) != 0
        for i in range(4):
            for j in range(4):
                a, b = src[x, rows(i, j), :], src[x, rows(7 - i, j), :]
                c, d = src[x, rows(i, 7 - j), :], src[x, rows(7 - i, 7 - j), :]
                a, b = jnp.where(flip_i, b, a), jnp.where(flip_i, a, b)
                c, d = jnp.where(flip_i, d, c), jnp.where(flip_i, c, d)
                mid[x, rows(i, j), :] = jnp.where(flip_j, c, a)
                mid[x, rows(i, 7 - j), :] = jnp.where(flip_j, a, c)
                mid[x, rows(7 - i, j), :] = jnp.where(flip_j, d, b)
                mid[x, rows(7 - i, 7 - j), :] = jnp.where(flip_j, b, d)
        for i in range(8):
            for k in range(4):
                a = mid[x, pl.ds(i * 64 + k, 8, stride=8), :]
                b = mid[x, pl.ds(i * 64 + 7 - k, 8, stride=8), :]
                out[x, pl.ds(i * 64 + k, 8, stride=8), :] = jnp.where(flip_k, b, a)
                out[x, pl.ds(i * 64 + 7 - k, 8, stride=8), :] = jnp.where(flip_k, a, b)


def start_kernel(ends, size_x_in, size_y_in, load_in, orient_in, size_z_in, *refs):
    field, y_low, y_high, x_low, x_high, coef, orient, mid, load, length_ref, x_ref, y_ref, ready = refs
    copies = [
        pltpu.make_async_copy(load_in.at[0], load.at[0], ready.at[0]),
        pltpu.make_async_copy(orient_in, orient, ready.at[1]),
        pltpu.make_async_copy(size_z_in, length_ref, ready.at[2]),
        pltpu.make_async_copy(size_x_in, x_ref, ready.at[3]),
        pltpu.make_async_copy(size_y_in, y_ref, ready.at[4]),
        pltpu.make_async_copy(load_in.at[1], load.at[1], ready.at[5]),
    ]
    for copy in copies:
        copy.start()
    for copy in copies[1:5]:
        copy.wait()
    node, dev = lax.axis_index("node"), lax.axis_index("dev")
    inside = [jnp.where(at_end, 0.0, 1.0).astype(F32) for at_end in (node == 0, node == ends[0], dev == 0, dev == ends[1])]
    size_y = y_ref[0]
    length = over_sublanes(length_ref[...])
    weight_k = sublane_table(WEIGHTS)
    lam_k = sublane_table(LAMS)
    at = lax.broadcasted_iota(jnp.int32, (8, 128), 0)
    for x in range(2):
        size_x = x_ref[x]
        coef_x = size_y * length / (2.0 * jnp.full((8, 128), size_x, F32))
        coef_y = size_x * length / (2.0 * jnp.full((8, 128), size_y, F32))
        coef_z = jnp.full((8, 128), size_x * size_y, F32) / (2.0 * length)
        coef[x, 0] = jnp.where(at == 0, coef_x, jnp.where(at == 1, coef_y, coef_z))
        coef[x, 1] = coef_x * weight_k
        coef[x, 2] = lam_k * coef_z + (coef_x + coef_y + coef_z) / 3.0
        coef[x, 3] = jnp.full((8, 128), inside[x], F32)
        coef[x, 4] = jnp.full((8, 128), inside[2 + x], F32)
        coef[x, 5] = weight_k
        coef[x, 6] = jnp.full((8, 128), jnp.where(dev % 2 == 1, 1.0, 0.0), F32)
    copies[0].wait()
    reversed_points(load, mid, field, orient, (0,))
    copies[5].wait()
    reversed_points(load, mid, field, orient, (1,))
    z_summed(field)
    x_joined(field)
    y_faces(field, y_low, y_high, coef)
    x_low[0:64, :] = field[0, plane(0), :]
    x_high[0:64, :] = field[1, plane(7), :]
    x_low[64:72, :] = coef[0, 0]
    x_high[64:72, :] = coef[1, 0]


def edge_kernel(coef, x_low, x_high, other, pair, low_out, high_out):
    low_out[...] = x_low[...]
    high_out[...] = x_high[...]
    low_out[0:8, :] += face_came(0, 0, 0, pair, other, coef)
    low_out[56:64, :] += face_came(0, 0, 7, pair, other, coef)
    high_out[0:8, :] += face_came(1, 7, 0, pair, other, coef)
    high_out[56:64, :] += face_came(1, 7, 7, pair, other, coef)


def solve_kernel(with_x, *refs):
    coef, table, field, before, after = refs[:5]
    refs = refs[5:]
    if with_x:
        x_before, x_after = refs[:2]
        refs = refs[2:]
    joined, out, y_low, y_high, dot, high, low, mid = refs
    for x in range(2):
        for pair in range(4):
            lines = []
            for j in (2 * pair, 2 * pair + 1):
                line = []
                for i in range(8):
                    value = y_joined(field[x, rows(i, j), :], x, i, j, before, after, coef)
                    if with_x and x == 0 and i == 0:
                        value = (value + x_before[eight(j), :]) * coef[0, 3] * (
                            coef[0, 4] if j == 0 else coef[1, 4] if j == 7 else 1.0
                        )
                    if with_x and x == 1 and i == 7:
                        value = (value + x_after[eight(j), :]) * coef[1, 3] * (
                            coef[0, 4] if j == 0 else coef[1, 4] if j == 7 else 1.0
                        )
                    joined[x, rows(i, j), :] = value
                    line.append(value)
                lines.append(to_modes(line))
            for m in range(8):
                store_split(high, low, m * 64 + pair * 16, lanes(x), [lines[0][m], lines[1][m]])
    for block in range(2):
        part = slice(block * 256, block * 256 + 256)
        mid[part, :] = product(table, 0, high[part, :], low[part, :])
    for x in range(2):
        coef_x, coef_y = over_sublanes(coef[x, 0, 0:1, :]), over_sublanes(coef[x, 0, 1:2, :])
        den_i = [coef_x * LAMS[m] for m in range(8)]
        den_j = [coef_y * LAMS[n] + coef[x, 2] for n in range(8)]
        for m in range(8):
            for pair in range(4):
                parts = [mid[rows(m, n), lanes(x)] / (den_i[m] + den_j[n]) for n in (2 * pair, 2 * pair + 1)]
                store_split(high, low, m * 64 + pair * 16, lanes(x), parts)
    for block in range(2):
        part = slice(block * 256, block * 256 + 256)
        mid[part, :] = product(table, 2, high[part, :], low[part, :])
    total = jnp.zeros((8, 128), F32)
    for x in range(2):
        for j in range(8):
            line = from_modes([mid[rows(m, j), lanes(x)] for m in range(8)])
            for i in range(8):
                out[x, rows(i, j), :] = line[i]
                total = total + line[i] * joined[x, rows(i, j), :]
    dot[...] = total
    z_summed(out)
    x_joined(out)
    y_faces(out, y_low, y_high, coef)


def local_kernel(coef, table, field, before, after, joined, out, x_low, x_high, high, low, first, second):
    for x in range(2):
        for pair in range(4):
            for i in range(8):
                parts = []
                for j in (2 * pair, 2 * pair + 1):
                    value = y_joined(field[x, rows(i, j), :], x, i, j, before, after, coef)
                    if x == 0 and i == 0:
                        value = value * coef[0, 3]
                    if x == 1 and i == 7:
                        value = value * coef[1, 3]
                    joined[x, rows(i, j), :] = value
                    parts.append(value)
                store_split(high, low, i * 64 + pair * 16, lanes(x), parts)
    for block in range(2):
        part = slice(block * 256, block * 256 + 256)
        first[part, :] = product(table, 0, high[part, :], low[part, :])
        second[part, :] = product(table, 2, high[part, :], low[part, :])
    for x in range(2):
        coef_y, coef_z = over_sublanes(coef[x, 0, 1:2, :]), over_sublanes(coef[x, 0, 2:3, :])
        for j in range(8):
            scale = coef[x, 1] * WEIGHTS[j]
            line = stiff_line([joined[x, rows(i, j), :] for i in range(8)])
            for i in range(8):
                flat = coef_y * first[rows(i, j), lanes(x)] + coef_z * second[rows(i, j), lanes(x)]
                out[x, rows(i, j), :] = scale * line[i] + WEIGHTS[i] * flat
    x_low[0:64, :] = joined[0, plane(0), :]
    x_low[64:128, :] = out[0, plane(0), :]
    x_high[0:64, :] = joined[1, plane(7), :]
    x_high[64:128, :] = out[1, plane(7), :]


def cross_kernel(with_row, *refs):
    coef, table, field, local, x_before, x_after, kind_before, kind_after = refs[:8]
    refs = refs[8:]
    if with_row:
        earlier = refs[:3]
        refs = refs[3:]
    joined, out, y_low, y_high, dot, high, low, first, second = refs
    joined[...] = field[...]
    for pair in range(4):
        parts = [[], [], [], []]
        for j in (2 * pair, 2 * pair + 1):
            for side in range(2):
                own = field[side, rows(7 * side, j), :]
                came = (x_after if side else x_before)[eight(j), :] * coef[side, 3]
                joined[side, rows(7 * side, j), :] = own + came
                parts[side].append(came)
                parts[2 + side].append(own)
        for n in range(4):
            store_split(high, low, n * 64 + pair * 16, slice(0, 128), parts[n])
    first[...] = product(table, 0, high[...], low[...])
    second[...] = product(table, 2, high[...], low[...])
    total = jnp.zeros((8, 128), F32)
    for side in range(2):
        end = 7 * side
        coef_y, coef_z = over_sublanes(coef[side, 0, 1:2, :]), over_sublanes(coef[side, 0, 2:3, :])
        kind, sent = (kind_after, x_after) if side else (kind_before, x_before)
        far_x, far_y, far_z = [over_sublanes(kind[64 + n : 65 + n, :]) for n in range(3)]
        for j in range(8):
            came = sent[eight(j), :] * coef[side, 3]
            own = field[side, rows(end, j), :]
            pulled = coef[side, 1] * WEIGHTS[j] * came
            for i in range(8):
                value = local[side, rows(i, j), :] + STIFF[i][end] * pulled
                if i == end:
                    flat = coef_y * first[rows(side, j), :] + coef_z * second[rows(side, j), :]
                    value = value + WEIGHTS[end] * flat
                total = total + value * joined[side, rows(i, j), :]
                if i == end:
                    far = sent[64 + j * 8 : 72 + j * 8, :]
                    far = far + (STIFF[7 - end][7 - end] * WEIGHTS[j]) * (far_x * coef[side, 5]) * own
                    flat = far_y * first[rows(2 + side, j), :] + far_z * second[rows(2 + side, j), :]
                    far = far + WEIGHTS[7 - end] * flat
                    value = (value + far) * coef[side, 3]
                out[side, rows(i, j), :] = value
    z_summed(out)
    x_joined(out)
    y_faces(out, y_low, y_high, coef)
    if with_row:
        lane = lax.broadcasted_iota(jnp.int32, (8, 128), 1)
        row = jnp.zeros((8, 128), F32)
        for n, value in enumerate([ref[...] for ref in earlier] + [total]):
            value = value + pltpu.roll(value, 64, 1)
            value = value + pltpu.roll(value, 32, 1)
            row = jnp.where(lane // 32 == n, value, row)
        row = over_sublanes(jnp.sum(row, axis=0, keepdims=True))
        for n in range(dot.shape[0] // 8):
            dot[eight(n), :] = row
    else:
        dot[...] = total


def sum_kernel(parts, out):
    row = over_sublanes(jnp.sum(parts[...], axis=0, keepdims=True))
    for n in range(out.shape[0] // 8):
        out[eight(n), :] = row


def end_kernel(coef, orient, sums, last, before, after, load, first, image, second, answer, rest, one, two, sent):
    lane = lax.broadcasted_iota(jnp.int32, (8, 128), 1)
    row = jnp.sum(sums[...], axis=0, keepdims=True)
    dots = [jnp.full((8, 128), jnp.sum(jnp.where(lane[0:1, :] // 32 == n, row, 0.0)), F32) for n in range(4)]
    alpha = dots[0] / dots[1]
    energy = dots[0] - 2.0 * alpha * dots[1] + alpha * alpha * dots[2]
    keep = 1.0 + energy / dots[0]
    curve = keep * keep * dots[1] - 2.0 * alpha * keep * dots[2] + alpha * alpha * dots[3]
    step = energy / curve
    on_first = alpha + step * keep
    on_second = step * alpha
    copies = []
    for x in range(2):
        for i in range(8):
            for j in range(8):
                at = rows(i, j)
                one[x, at, :] = on_first * first[x, at, :] - on_second * second[x, at, :]
        reversed_points(one, one, one, orient, (x,))
        copies.append(pltpu.make_async_copy(one.at[x], answer.at[x], sent.at[x, 0]))
        copies[-1].start()
        for i in range(8):
            for j in range(8):
                at = rows(i, j)
                value = y_joined(last[x, at, :], x, i, j, before, after, coef)
                two[x, at, :] = load[x, at, :] - on_first * image[x, at, :] + on_second * value
        reversed_points(two, two, two, orient, (x,))
        copies.append(pltpu.make_async_copy(two.at[x], rest.at[x], sent.at[x, 1]))
        copies[-1].start()
    for copy in copies:
        copy.wait()


def f32(*shape):
    return jax.ShapeDtypeStruct(shape, F32)


def call(kernel, outs, scratch, *args, spaces=(), room=24, out_space=pltpu.VMEM):
    return pl.pallas_call(
        kernel,
        out_shape=outs,
        in_specs=[pl.BlockSpec(memory_space=space) for space in spaces]
        + [pl.BlockSpec(memory_space=pltpu.VMEM)] * (len(args) - len(spaces)),
        out_specs=jax.tree.map(lambda _: pl.BlockSpec(memory_space=out_space), outs),
        scratch_shapes=scratch,
        compiler_params=pltpu.CompilerParams(vmem_limit_bytes=room * 1024 * 1024),
    )(*args)


FIELD = f32(2, 512, 128)
FACES = [f32(2, 64, 128)] * 2
EIGHT = f32(8, 128)


def kept_in_hbm(x):
    return pltpu.with_memory_space_constraint(x, pltpu.HBM)


def swap_y(pair, other):
    devs = lax.axis_size("dev")
    far = lax.ppermute(other, "dev", [(i, i - 1 if i % 2 == 0 else i + 1) for i in range(1, devs - 1)])
    near = lax.ppermute(pair, "dev", [(i, i + 1 if i % 2 == 0 else i - 1) for i in range(devs)])
    return far, near


def swap_x(low, high):
    return passed_along(high, "node", 1), passed_along(low, "node", -1)


def exchanged(rows_out, axis):
    came = lax.all_to_all(rows_out.reshape(-1, 1, 128), axis, 0, 0)
    return came.reshape(rows_out.shape)


def shards(element_load, orient, size_x, size_y, size_z):
    solve_np, local_np = plane_tables()
    solve_table, local_table = jnp.asarray(solve_np), jnp.asarray(local_np)
    nodes, devs = lax.axis_size("node"), lax.axis_size("dev")
    field, y_low, y_high, x_low, x_high, coef, orient = call(
        functools.partial(start_kernel, (nodes - 1, devs - 1)),
        [FIELD, *FACES, f32(72, 128), f32(72, 128), f32(2, 8, 8, 128), jax.ShapeDtypeStruct((2, 128), jnp.int32)],
        [
            pltpu.VMEM((2, 512, 128), F32),
            pltpu.VMEM((2, 512, 128), F32),
            pltpu.VMEM((1, 128), F32),
            pltpu.SMEM((2,), F32),
            pltpu.SMEM((1,), F32),
            pltpu.SemaphoreType.DMA((6,)),
        ],
        kept_in_hbm(size_x), size_y,
        *map(kept_in_hbm, (element_load.reshape(2, 512, 128), orient.reshape(2, 128), size_z.reshape(1, 128))),
        spaces=[pltpu.HBM] * 5,
    )
    y_came = swap_y(y_low, y_high)
    x_faces = call(edge_kernel, [f32(72, 128)] * 2, [], coef, x_low, x_high, *y_came)
    kinds = swap_x(*x_faces)

    def solved(field, y_came, x_came):
        joined, out, low, high, dot = call(
            functools.partial(solve_kernel, bool(x_came)),
            [FIELD, FIELD, *FACES, EIGHT],
            [pltpu.VMEM((512, 256), BF16)] * 2 + [pltpu.VMEM((512, 256), F32)],
            coef, solve_table, field, *y_came, *x_came,
        )
        return joined, out, swap_y(low, high), dot

    def applied(field, y_came, earlier):
        joined, local, low, high = call(
            local_kernel,
            [FIELD, FIELD, f32(128, 128), f32(128, 128)],
            [pltpu.VMEM((512, 256), BF16)] * 2 + [pltpu.VMEM((512, 256), F32)] * 2,
            coef, local_table, field, *y_came,
        )
        x_came = swap_x(low, high)
        joined, out, low, high, dot = call(
            functools.partial(cross_kernel, bool(earlier)),
            [FIELD, FIELD, *FACES, pltpu.VMEM((8, 128), F32) if earlier else EIGHT],
            [pltpu.VMEM((256, 128), BF16)] * 2 + [pltpu.VMEM((256, 128), F32)] * 2,
            coef, local_table, joined, local, *x_came, *kinds, *earlier,
        )
        return joined, out, (low, high), dot

    load, out, y_came, dot_a = solved(field, y_came, kinds)
    first, out, faces, dot_c = applied(out, y_came, ())
    image, out, y_came, dot_d = solved(out, swap_y(*faces), ())
    second, out, (low, high), row = applied(out, y_came, (dot_a, dot_c, dot_d))
    before, after = swap_y(low, high)
    row = call(sum_kernel, pltpu.VMEM((64, 128), F32), [], exchanged(row, "node"))
    row = exchanged(row, "dev")
    answer, rest = call(
        end_kernel,
        [FIELD, FIELD],
        [pltpu.VMEM((2, 512, 128), F32)] * 2 + [pltpu.SemaphoreType.DMA((2, 2))],
        coef, orient, row, out, before, after, load, first, image, second,
        out_space=pltpu.HBM,
    )
    return answer.reshape(element_load.shape), rest.reshape(element_load.shape)


def solution(mesh):
    return jax.shard_map(
        shards,
        mesh=mesh,
        in_specs=(
            P("node", "dev", None, None, None, None),
            P("node", "dev", None),
            P("node"),
            P("dev"),
            P(),
        ),
        out_specs=(
            P("node", "dev", None, None, None, None),
            P("node", "dev", None, None, None, None),
        ),
        check_vma=False,
    )
```

```python
import functools
import math

import jax
import jax.numpy as jnp
import ml_dtypes
import numpy as np
from jax import lax
from jax.experimental import pallas as pl
from jax.experimental.pallas import tpu as pltpu
from jax.sharding import PartitionSpec as P

F32 = jnp.float32
BF16 = jnp.bfloat16


def passed_along(x, axis, by):
    peers = lax.axis_size(axis)
    return lax.ppermute(x, axis, [(i, (i + by) % peers) for i in range(peers)])


def legendre_pair(value):
    prev_val = 1.0
    curr_val = value
    prev_der = 0.0
    curr_der = 1.0
    for order in range(2, 8):
        next_val = ((2 * order - 1) * value * curr_val - (order - 1) * prev_val) / order
        next_der = prev_der + (2 * order - 1) * curr_val
        prev_val, curr_val = (curr_val, next_val)
        prev_der, curr_der = (curr_der, next_der)
    return (curr_val, curr_der)


def second_derivative(value):
    leg_val, leg_der = legendre_pair(value)
    return (2.0 * value * leg_der - 56.0 * leg_val) / (1.0 - value * value)


def basis_tables():
    guesses = [
        -0.8717401485096066,
        -0.5917001814331423,
        -0.2092992179024789,
        0.2092992179024789,
        0.5917001814331423,
        0.8717401485096066,
    ]
    inner_pts = []
    for guess in guesses:
        point = guess
        for newton in range(4):
            point = point - legendre_pair(point)[1] / second_derivative(point)
        inner_pts.append(point)
    gll_points = [-1.0] + inner_pts + [1.0]
    leg_values = [legendre_pair(point)[0] for point in gll_points]
    weights = [2.0 / (56.0 * lv * lv) for lv in leg_values]
    derivative = [[0.0] * 8 for row_at in range(8)]
    for row_at in range(8):
        for col_at in range(8):
            if row_at != col_at:
                derivative[row_at][col_at] = leg_values[row_at] / (
                    leg_values[col_at] * (gll_points[row_at] - gll_points[col_at])
                )
    derivative[0][0] = -14.0
    derivative[7][7] = 14.0
    stiffness = [
        [
            sum(
                (
                    derivative[mid][row_at] * weights[mid] * derivative[mid][col_at]
                    for mid in range(8)
                )
            )
            for col_at in range(8)
        ]
        for row_at in range(8)
    ]
    inv_sqrt = [1.0 / math.sqrt(wt) for wt in weights]
    matrix = [
        [inv_sqrt[row_at] * stiffness[row_at][col_at] * inv_sqrt[col_at] for col_at in range(8)]
        for row_at in range(8)
    ]
    vectors = [[1.0 if row_at == col_at else 0.0 for col_at in range(8)] for row_at in range(8)]
    for sweep in range(14):
        for first in range(8):
            for second in range(first + 1, 8):
                angle = 0.5 * math.atan2(
                    2.0 * matrix[first][second], matrix[second][second] - matrix[first][first]
                )
                cosine = math.cos(angle)
                sine = math.sin(angle)
                for other in range(8):
                    left_val = matrix[other][first]
                    right_val = matrix[other][second]
                    matrix[other][first] = cosine * left_val - sine * right_val
                    matrix[other][second] = sine * left_val + cosine * right_val
                for other in range(8):
                    left_val = matrix[first][other]
                    right_val = matrix[second][other]
                    matrix[first][other] = cosine * left_val - sine * right_val
                    matrix[second][other] = sine * left_val + cosine * right_val
                for other in range(8):
                    left_val = vectors[other][first]
                    right_val = vectors[other][second]
                    vectors[other][first] = cosine * left_val - sine * right_val
                    vectors[other][second] = sine * left_val + cosine * right_val
    eigen_vals = [max(matrix[idx_at][idx_at], 0.0) for idx_at in range(8)]
    eigen_modes = [
        [inv_sqrt[row_at] * vectors[row_at][col_at] for col_at in range(8)] for row_at in range(8)
    ]
    return (weights, stiffness, eigen_modes, eigen_vals)


WEIGHTS, STIFF, MODES, LAMS = basis_tables()
EVEN = [MODES[0][m] * MODES[7][m] > 0 for m in range(8)]


def split_table(table):
    high = table.astype(ml_dtypes.bfloat16)
    low = (table - high.astype(np.float64)).astype(ml_dtypes.bfloat16)
    return [high, low]


def plane_tables():
    modes, stiff, weights = np.array(MODES), np.array(STIFF), np.diag(WEIGHTS)
    four = np.eye(4)
    forward = np.kron(four, np.kron(modes.T, modes.T))
    backward = np.kron(four, np.kron(modes, modes))
    along_j = np.kron(four, np.kron(stiff, weights))
    along_k = np.kron(four, np.kron(weights, stiff))
    solve = np.stack(split_table(forward) + split_table(backward))
    local = np.stack(split_table(along_j) + split_table(along_k))
    return solve, local


def rows(i, j):
    return slice((i * 8 + j) * 8, (i * 8 + j) * 8 + 8)


def plane(n):
    return slice(n * 64, n * 64 + 64)


def eight(n):
    return slice(n * 8, n * 8 + 8)


def lanes(x):
    return slice(x * 128, x * 128 + 128)


def weighted(values, factors):
    total = None
    for value, factor in zip(values, factors):
        term = value * factor
        total = term if total is None else total + term
    return total


def halves(v):
    return [v[a] + v[7 - a] for a in range(4)], [v[a] - v[7 - a] for a in range(4)]


def to_modes(v):
    even, odd = halves(v)
    return [weighted(even if EVEN[m] else odd, [MODES[a][m] for a in range(4)]) for m in range(8)]


def from_modes(t):
    out = [None] * 8
    for a in range(4):
        even = weighted([t[m] for m in range(8) if EVEN[m]], [MODES[a][m] for m in range(8) if EVEN[m]])
        odd = weighted([t[m] for m in range(8) if not EVEN[m]], [MODES[a][m] for m in range(8) if not EVEN[m]])
        out[a], out[7 - a] = even + odd, even - odd
    return out


def stiff_line(v):
    even, odd = halves(v)
    out = [None] * 8
    for i in range(4):
        first = weighted(even, [0.5 * (STIFF[i][a] + STIFF[i][7 - a]) for a in range(4)])
        second = weighted(odd, [0.5 * (STIFF[i][a] - STIFF[i][7 - a]) for a in range(4)])
        out[i], out[7 - i] = first + second, first - second
    return out


def store_split(high_ref, low_ref, row, column, parts):
    chunk = jnp.concatenate(parts, axis=0)
    high = chunk.astype(BF16)
    low = (chunk - high.astype(F32)).astype(BF16)
    high_ref[row : row + 16, column] = high
    low_ref[row : row + 16, column] = low


def product(table, at, high, low):
    dot = functools.partial(jnp.dot, preferred_element_type=F32)
    return dot(table[at], high) + dot(table[at], low) + dot(table[at + 1], high)


def z_summed(ref):
    lane = lax.broadcasted_iota(jnp.int32, (8, 128), 1)
    for x in range(2):
        for i in range(8):
            first = ref[x, pl.ds(i * 64, 8, stride=8), :]
            last = ref[x, pl.ds(i * 64 + 7, 8, stride=8), :]
            ref[x, pl.ds(i * 64, 8, stride=8), :] = jnp.where(lane == 0, 0.0, first + pltpu.roll(last, 1, 1))
            ref[x, pl.ds(i * 64 + 7, 8, stride=8), :] = jnp.where(lane == 127, 0.0, last + pltpu.roll(first, 127, 1))


def x_joined(ref):
    both = ref[0, plane(7), :] + ref[1, plane(0), :]
    ref[0, plane(7), :] = both
    ref[1, plane(0), :] = both


def is_odd(coef):
    return coef[0, 6] > 0.5


def y_faces(ref, pair_ref, other_ref, coef):
    odd = is_odd(coef)
    for x in range(2):
        for i in range(8):
            low, high = ref[x, rows(i, 0), :], ref[x, rows(i, 7), :]
            pair_ref[x, eight(i), :] = jnp.where(odd, low, high)
            other_ref[x, eight(i), :] = jnp.where(odd, high, low)


def face_came(x, i, end, pair, other, coef):
    odd = is_odd(coef)
    first, second = (other, pair) if end == 0 else (pair, other)
    return jnp.where(odd, second[x, eight(i), :], first[x, eight(i), :])


def y_joined(value, x, i, j, other, pair, coef):
    if j == 0:
        value = (value + face_came(x, i, 0, pair, other, coef)) * coef[0, 4]
    if j == 7:
        value = (value + face_came(x, i, 7, pair, other, coef)) * coef[1, 4]
    return value


def sublane_table(values):
    at = lax.broadcasted_iota(jnp.int32, (8, 128), 0)
    out = jnp.full((8, 128), values[7], F32)
    for n in range(7):
        out = jnp.where(at == n, values[n], out)
    return out


def over_sublanes(row):
    return jnp.broadcast_to(row, (8, 128))


def reversed_points(src, mid, out, orient, columns=(0, 1)):
    for x in columns:
        code = over_sublanes(orient[x : x + 1, :])
        flip_i, flip_j, flip_k = (code & 1) != 0, (code & 2) != 0, (code & 4) != 0
        for i in range(4):
            for j in range(4):
                a, b = src[x, rows(i, j), :], src[x, rows(7 - i, j), :]
                c, d = src[x, rows(i, 7 - j), :], src[x, rows(7 - i, 7 - j), :]
                a, b = jnp.where(flip_i, b, a), jnp.where(flip_i, a, b)
                c, d = jnp.where(flip_i, d, c), jnp.where(flip_i, c, d)
                mid[x, rows(i, j), :] = jnp.where(flip_j, c, a)
                mid[x, rows(i, 7 - j), :] = jnp.where(flip_j, a, c)
                mid[x, rows(7 - i, j), :] = jnp.where(flip_j, d, b)
                mid[x, rows(7 - i, 7 - j), :] = jnp.where(flip_j, b, d)
        for i in range(8):
            for k in range(4):
                a = mid[x, pl.ds(i * 64 + k, 8, stride=8), :]
                b = mid[x, pl.ds(i * 64 + 7 - k, 8, stride=8), :]
                out[x, pl.ds(i * 64 + k, 8, stride=8), :] = jnp.where(flip_k, b, a)
                out[x, pl.ds(i * 64 + 7 - k, 8, stride=8), :] = jnp.where(flip_k, a, b)


def start_kernel(ends, size_x_in, size_y_in, load_in, orient_in, size_z_in, *refs):
    field, y_low, y_high, x_low, x_high, coef, orient, mid, load, length_ref, x_ref, y_ref, ready = refs
    copies = [
        pltpu.make_async_copy(load_in.at[0], load.at[0], ready.at[0]),
        pltpu.make_async_copy(orient_in, orient, ready.at[1]),
        pltpu.make_async_copy(size_z_in, length_ref, ready.at[2]),
        pltpu.make_async_copy(size_x_in, x_ref, ready.at[3]),
        pltpu.make_async_copy(size_y_in, y_ref, ready.at[4]),
        pltpu.make_async_copy(load_in.at[1], load.at[1], ready.at[5]),
    ]
    for copy in copies:
        copy.start()
    for copy in copies[1:5]:
        copy.wait()
    node, dev = lax.axis_index("node"), lax.axis_index("dev")
    inside = [jnp.where(at_end, 0.0, 1.0).astype(F32) for at_end in (node == 0, node == ends[0], dev == 0, dev == ends[1])]
    size_y = y_ref[0]
    length = over_sublanes(length_ref[...])
    weight_k = sublane_table(WEIGHTS)
    lam_k = sublane_table(LAMS)
    at = lax.broadcasted_iota(jnp.int32, (8, 128), 0)
    for x in range(2):
        size_x = x_ref[x]
        coef_x = size_y * length / (2.0 * jnp.full((8, 128), size_x, F32))
        coef_y = size_x * length / (2.0 * jnp.full((8, 128), size_y, F32))
        coef_z = jnp.full((8, 128), size_x * size_y, F32) / (2.0 * length)
        coef[x, 0] = jnp.where(at == 0, coef_x, jnp.where(at == 1, coef_y, coef_z))
        coef[x, 1] = coef_x * weight_k
        coef[x, 2] = lam_k * coef_z + (coef_x + coef_y + coef_z) / 3.0
        coef[x, 3] = jnp.full((8, 128), inside[x], F32)
        coef[x, 4] = jnp.full((8, 128), inside[2 + x], F32)
        coef[x, 5] = weight_k
        coef[x, 6] = jnp.full((8, 128), jnp.where(dev % 2 == 1, 1.0, 0.0), F32)
    copies[0].wait()
    reversed_points(load, mid, field, orient, (0,))
    copies[5].wait()
    reversed_points(load, mid, field, orient, (1,))
    z_summed(field)
    x_joined(field)
    y_faces(field, y_low, y_high, coef)
    x_low[0:64, :] = field[0, plane(0), :]
    x_high[0:64, :] = field[1, plane(7), :]
    x_low[64:72, :] = coef[0, 0]
    x_high[64:72, :] = coef[1, 0]


def edge_kernel(coef, x_low, x_high, other, pair, low_out, high_out):
    low_out[...] = x_low[...]
    high_out[...] = x_high[...]
    low_out[0:8, :] += face_came(0, 0, 0, pair, other, coef)
    low_out[56:64, :] += face_came(0, 0, 7, pair, other, coef)
    high_out[0:8, :] += face_came(1, 7, 0, pair, other, coef)
    high_out[56:64, :] += face_came(1, 7, 7, pair, other, coef)


def solve_kernel(with_x, *refs):
    coef, table, field, before, after = refs[:5]
    refs = refs[5:]
    if with_x:
        x_before, x_after = refs[:2]
        refs = refs[2:]
    joined, out, y_low, y_high, dot, high, low, mid = refs
    for x in range(2):
        for pair in range(4):
            lines = []
            for j in (2 * pair, 2 * pair + 1):
                line = []
                for i in range(8):
                    value = y_joined(field[x, rows(i, j), :], x, i, j, before, after, coef)
                    if with_x and x == 0 and i == 0:
                        value = (value + x_before[eight(j), :]) * coef[0, 3] * (
                            coef[0, 4] if j == 0 else coef[1, 4] if j == 7 else 1.0
                        )
                    if with_x and x == 1 and i == 7:
                        value = (value + x_after[eight(j), :]) * coef[1, 3] * (
                            coef[0, 4] if j == 0 else coef[1, 4] if j == 7 else 1.0
                        )
                    joined[x, rows(i, j), :] = value
                    line.append(value)
                lines.append(to_modes(line))
            for m in range(8):
                store_split(high, low, m * 64 + pair * 16, lanes(x), [lines[0][m], lines[1][m]])
    for block in range(2):
        part = slice(block * 256, block * 256 + 256)
        mid[part, :] = product(table, 0, high[part, :], low[part, :])
    for x in range(2):
        coef_x, coef_y = over_sublanes(coef[x, 0, 0:1, :]), over_sublanes(coef[x, 0, 1:2, :])
        den_i = [coef_x * LAMS[m] for m in range(8)]
        den_j = [coef_y * LAMS[n] + coef[x, 2] for n in range(8)]
        for m in range(8):
            for pair in range(4):
                parts = [mid[rows(m, n), lanes(x)] / (den_i[m] + den_j[n]) for n in (2 * pair, 2 * pair + 1)]
                store_split(high, low, m * 64 + pair * 16, lanes(x), parts)
    for block in range(2):
        part = slice(block * 256, block * 256 + 256)
        mid[part, :] = product(table, 2, high[part, :], low[part, :])
    total = jnp.zeros((8, 128), F32)
    for x in range(2):
        for j in range(8):
            line = from_modes([mid[rows(m, j), lanes(x)] for m in range(8)])
            for i in range(8):
                out[x, rows(i, j), :] = line[i]
                total = total + line[i] * joined[x, rows(i, j), :]
    dot[...] = total
    z_summed(out)
    x_joined(out)
    y_faces(out, y_low, y_high, coef)


def local_kernel(coef, table, field, before, after, joined, out, x_low, x_high, high, low, first, second):
    for x in range(2):
        for pair in range(4):
            for i in range(8):
                parts = []
                for j in (2 * pair, 2 * pair + 1):
                    value = y_joined(field[x, rows(i, j), :], x, i, j, before, after, coef)
                    if x == 0 and i == 0:
                        value = value * coef[0, 3]
                    if x == 1 and i == 7:
                        value = value * coef[1, 3]
                    joined[x, rows(i, j), :] = value
                    parts.append(value)
                store_split(high, low, i * 64 + pair * 16, lanes(x), parts)
    for block in range(2):
        part = slice(block * 256, block * 256 + 256)
        first[part, :] = product(table, 0, high[part, :], low[part, :])
        second[part, :] = product(table, 2, high[part, :], low[part, :])
    for x in range(2):
        coef_y, coef_z = over_sublanes(coef[x, 0, 1:2, :]), over_sublanes(coef[x, 0, 2:3, :])
        for j in range(8):
            scale = coef[x, 1] * WEIGHTS[j]
            line = stiff_line([joined[x, rows(i, j), :] for i in range(8)])
            for i in range(8):
                flat = coef_y * first[rows(i, j), lanes(x)] + coef_z * second[rows(i, j), lanes(x)]
                out[x, rows(i, j), :] = scale * line[i] + WEIGHTS[i] * flat
    x_low[0:64, :] = joined[0, plane(0), :]
    x_low[64:128, :] = out[0, plane(0), :]
    x_high[0:64, :] = joined[1, plane(7), :]
    x_high[64:128, :] = out[1, plane(7), :]


def cross_kernel(with_row, *refs):
    coef, table, field, local, x_before, x_after, kind_before, kind_after = refs[:8]
    refs = refs[8:]
    if with_row:
        earlier = refs[:3]
        refs = refs[3:]
    joined, out, y_low, y_high, dot, high, low, first, second = refs
    joined[...] = field[...]
    for pair in range(4):
        parts = [[], [], [], []]
        for j in (2 * pair, 2 * pair + 1):
            for side in range(2):
                own = field[side, rows(7 * side, j), :]
                came = (x_after if side else x_before)[eight(j), :] * coef[side, 3]
                joined[side, rows(7 * side, j), :] = own + came
                parts[side].append(came)
                parts[2 + side].append(own)
        for n in range(4):
            store_split(high, low, n * 64 + pair * 16, slice(0, 128), parts[n])
    first[...] = product(table, 0, high[...], low[...])
    second[...] = product(table, 2, high[...], low[...])
    total = jnp.zeros((8, 128), F32)
    for side in range(2):
        end = 7 * side
        coef_y, coef_z = over_sublanes(coef[side, 0, 1:2, :]), over_sublanes(coef[side, 0, 2:3, :])
        kind, sent = (kind_after, x_after) if side else (kind_before, x_before)
        far_x, far_y, far_z = [over_sublanes(kind[64 + n : 65 + n, :]) for n in range(3)]
        for j in range(8):
            came = sent[eight(j), :] * coef[side, 3]
            own = field[side, rows(end, j), :]
            pulled = coef[side, 1] * WEIGHTS[j] * came
            for i in range(8):
                value = local[side, rows(i, j), :] + STIFF[i][end] * pulled
                if i == end:
                    flat = coef_y * first[rows(side, j), :] + coef_z * second[rows(side, j), :]
                    value = value + WEIGHTS[end] * flat
                total = total + value * joined[side, rows(i, j), :]
                if i == end:
                    far = sent[64 + j * 8 : 72 + j * 8, :]
                    far = far + (STIFF[7 - end][7 - end] * WEIGHTS[j]) * (far_x * coef[side, 5]) * own
                    flat = far_y * first[rows(2 + side, j), :] + far_z * second[rows(2 + side, j), :]
                    far = far + WEIGHTS[7 - end] * flat
                    value = (value + far) * coef[side, 3]
                out[side, rows(i, j), :] = value
    z_summed(out)
    x_joined(out)
    y_faces(out, y_low, y_high, coef)
    if with_row:
        lane = lax.broadcasted_iota(jnp.int32, (8, 128), 1)
        row = jnp.zeros((8, 128), F32)
        for n, value in enumerate([ref[...] for ref in earlier] + [total]):
            value = value + pltpu.roll(value, 64, 1)
            value = value + pltpu.roll(value, 32, 1)
            row = jnp.where(lane // 32 == n, value, row)
        row = over_sublanes(jnp.sum(row, axis=0, keepdims=True))
        for n in range(dot.shape[0] // 8):
            dot[eight(n), :] = row
    else:
        dot[...] = total


def sum_kernel(parts, out):
    row = over_sublanes(jnp.sum(parts[...], axis=0, keepdims=True))
    for n in range(out.shape[0] // 8):
        out[eight(n), :] = row


def end_kernel(coef, orient, sums, last, before, after, load, first, image, second, answer, rest, one, two, sent):
    lane = lax.broadcasted_iota(jnp.int32, (8, 128), 1)
    row = jnp.sum(sums[...], axis=0, keepdims=True)
    dots = [jnp.full((8, 128), jnp.sum(jnp.where(lane[0:1, :] // 32 == n, row, 0.0)), F32) for n in range(4)]
    alpha = dots[0] / dots[1]
    energy = dots[0] - 2.0 * alpha * dots[1] + alpha * alpha * dots[2]
    keep = 1.0 + energy / dots[0]
    curve = keep * keep * dots[1] - 2.0 * alpha * keep * dots[2] + alpha * alpha * dots[3]
    step = energy / curve
    on_first = alpha + step * keep
    on_second = step * alpha
    copies = []
    for x in range(2):
        for i in range(8):
            for j in range(8):
                at = rows(i, j)
                one[x, at, :] = on_first * first[x, at, :] - on_second * second[x, at, :]
        reversed_points(one, one, one, orient, (x,))
        copies.append(pltpu.make_async_copy(one.at[x], answer.at[x], sent.at[x, 0]))
        copies[-1].start()
        for i in range(8):
            for j in range(8):
                at = rows(i, j)
                value = y_joined(last[x, at, :], x, i, j, before, after, coef)
                two[x, at, :] = load[x, at, :] - on_first * image[x, at, :] + on_second * value
        reversed_points(two, two, two, orient, (x,))
        copies.append(pltpu.make_async_copy(two.at[x], rest.at[x], sent.at[x, 1]))
        copies[-1].start()
    for copy in copies:
        copy.wait()


def f32(*shape):
    return jax.ShapeDtypeStruct(shape, F32)


def call(kernel, outs, scratch, *args, spaces=(), room=24, out_space=pltpu.VMEM):
    return pl.pallas_call(
        kernel,
        out_shape=outs,
        in_specs=[pl.BlockSpec(memory_space=space) for space in spaces]
        + [pl.BlockSpec(memory_space=pltpu.VMEM)] * (len(args) - len(spaces)),
        out_specs=jax.tree.map(lambda _: pl.BlockSpec(memory_space=out_space), outs),
        scratch_shapes=scratch,
        compiler_params=pltpu.CompilerParams(vmem_limit_bytes=room * 1024 * 1024),
    )(*args)


FIELD = f32(2, 512, 128)
FACES = [f32(2, 64, 128)] * 2
EIGHT = f32(8, 128)


def kept_in_hbm(x):
    return pltpu.with_memory_space_constraint(x, pltpu.HBM)


def swap_y(pair, other):
    devs = lax.axis_size("dev")
    far = lax.ppermute(other, "dev", [(i, i - 1 if i % 2 == 0 else i + 1) for i in range(1, devs - 1)])
    near = lax.ppermute(pair, "dev", [(i, i + 1 if i % 2 == 0 else i - 1) for i in range(devs)])
    return far, near


def swap_x(low, high):
    return passed_along(high, "node", 1), passed_along(low, "node", -1)


Y_CHIPS = 4


def plane_groups():
    nodes, devs = lax.axis_size("node"), lax.axis_size("dev")
    return [[n * devs + z + y for n in range(nodes) for y in range(Y_CHIPS)] for z in range(0, devs, Y_CHIPS)]


def column_groups():
    nodes, devs = lax.axis_size("node"), lax.axis_size("dev")
    return [[n * devs + z + y for z in range(0, devs, Y_CHIPS)] for n in range(nodes) for y in range(Y_CHIPS)]


def exchanged(rows_out, groups):
    came = lax.all_to_all(rows_out.reshape(-1, 1, 128), ("node", "dev"), 0, 0, axis_index_groups=groups)
    return came.reshape(rows_out.shape)


def shards(element_load, orient, size_x, size_y, size_z):
    solve_np, local_np = plane_tables()
    solve_table, local_table = jnp.asarray(solve_np), jnp.asarray(local_np)
    nodes, devs = lax.axis_size("node"), lax.axis_size("dev")
    field, y_low, y_high, x_low, x_high, coef, orient = call(
        functools.partial(start_kernel, (nodes - 1, devs - 1)),
        [FIELD, *FACES, f32(72, 128), f32(72, 128), f32(2, 8, 8, 128), jax.ShapeDtypeStruct((2, 128), jnp.int32)],
        [
            pltpu.VMEM((2, 512, 128), F32),
            pltpu.VMEM((2, 512, 128), F32),
            pltpu.VMEM((1, 128), F32),
            pltpu.SMEM((2,), F32),
            pltpu.SMEM((1,), F32),
            pltpu.SemaphoreType.DMA((6,)),
        ],
        kept_in_hbm(size_x), size_y,
        *map(kept_in_hbm, (element_load.reshape(2, 512, 128), orient.reshape(2, 128), size_z.reshape(1, 128))),
        spaces=[pltpu.HBM] * 5,
    )
    y_came = swap_y(y_low, y_high)
    x_faces = call(edge_kernel, [f32(72, 128)] * 2, [], coef, x_low, x_high, *y_came)
    kinds = swap_x(*x_faces)

    def solved(field, y_came, x_came):
        joined, out, low, high, dot = call(
            functools.partial(solve_kernel, bool(x_came)),
            [FIELD, FIELD, *FACES, EIGHT],
            [pltpu.VMEM((512, 256), BF16)] * 2 + [pltpu.VMEM((512, 256), F32)],
            coef, solve_table, field, *y_came, *x_came,
        )
        return joined, out, swap_y(low, high), dot

    def applied(field, y_came, earlier):
        joined, local, low, high = call(
            local_kernel,
            [FIELD, FIELD, f32(128, 128), f32(128, 128)],
            [pltpu.VMEM((512, 256), BF16)] * 2 + [pltpu.VMEM((512, 256), F32)] * 2,
            coef, local_table, field, *y_came,
        )
        x_came = swap_x(low, high)
        joined, out, low, high, dot = call(
            functools.partial(cross_kernel, bool(earlier)),
            [FIELD, FIELD, *FACES, pltpu.VMEM((32, 128), F32) if earlier else EIGHT],
            [pltpu.VMEM((256, 128), BF16)] * 2 + [pltpu.VMEM((256, 128), F32)] * 2,
            coef, local_table, joined, local, *x_came, *kinds, *earlier,
        )
        return joined, out, (low, high), dot

    load, out, y_came, dot_a = solved(field, y_came, kinds)
    first, out, faces, dot_c = applied(out, y_came, ())
    image, out, y_came, dot_d = solved(out, swap_y(*faces), ())
    second, out, (low, high), row = applied(out, y_came, (dot_a, dot_c, dot_d))
    before, after = swap_y(low, high)
    row = call(sum_kernel, pltpu.VMEM((16, 128), F32), [], exchanged(row, plane_groups()))
    row = exchanged(row, column_groups())
    answer, rest = call(
        end_kernel,
        [FIELD, FIELD],
        [pltpu.VMEM((2, 512, 128), F32)] * 2 + [pltpu.SemaphoreType.DMA((2, 2))],
        coef, orient, row, out, before, after, load, first, image, second,
        out_space=pltpu.HBM,
    )
    return answer.reshape(element_load.shape), rest.reshape(element_load.shape)


def solution(mesh):
    return jax.shard_map(
        shards,
        mesh=mesh,
        in_specs=(
            P("node", "dev", None, None, None, None),
            P("node", "dev", None),
            P("node"),
            P("dev"),
            P(),
        ),
        out_specs=(
            P("node", "dev", None, None, None, None),
            P("node", "dev", None, None, None, None),
        ),
        check_vma=False,
    )
```
